256 devices in a mesh: rows: 32 (over z_hi, y, x), cols: 8 (over z_lo, core).
Axes of the slice: x: 4, y: 4, z: 8 (z_hi: 2, z_lo: 4; z = z_hi * 4 + z_lo), core: 2. Of those that a mesh axis runs over, the one named last changes fastest.
Arguments:
- logged: bfloat16 [32768, 256], P(('rows', 'cols')), may hold values from -8 to 8
- fresh: bfloat16 [65536, 256], P(('cols', 'rows')), may hold values from -6 to 6
- warm: float32 [65536], P('cols'), may hold values from -1 to 1
Outputs:
- row_potential: float32 [32768], P('rows')
- col_potential: float32 [65536], P('cols')
- reward: float32 [32768], P('rows')
The draws below stay inside these ranges and needn't reach their ends.
All inputs are finite; a program needn't handle non-finite values.
Results may differ from the reference program's by a relative error of at most 0.0013.
Values may be sent and summed in bfloat16 or wider, within the bound.
No kernel may reach another device: no remote copies, remote signals or barrier semaphores. Data moves between devices by JAX's collectives and lax.ppermute only.
A program may use at most 128 MiB of HBM per device.

```python
import jax
import jax.numpy as jnp
from jax import lax

E = 256
R_DEV = 1024
N = 32768
M = 65536


def draw_logged(key, part):
    key = jax.random.fold_in(key, 7)
    first, second = jax.random.split(key)
    base = jax.random.normal(first, (N, E), jnp.float32)
    scale = jnp.exp(jax.random.uniform(second, (N, 1), jnp.float32, jnp.log(0.7), jnp.log(1.4)))
    return jnp.clip(base * scale, -8.0, 8.0).astype(jnp.bfloat16)


def levels(key, dims, cuts, low, high):
    def one(position, blocks):
        heights = jax.random.uniform(jax.random.fold_in(jax.random.fold_in(key, 6), position), (blocks,), jnp.float32, low / len(cuts), high / len(cuts))
        return jnp.repeat(jnp.exp(heights), dims[position] // blocks).reshape((-1,) + (1,) * (len(dims) - position - 1))

    factor_of = one(*cuts[0])
    for cut in cuts[1:]:
        factor_of = factor_of * one(*cut)
    return factor_of


def normal_values(rng, extent, deviation, limit, cuts=(), held_as=jnp.bfloat16):
    loudness = levels(rng, extent, cuts, -0.22, 0.18) if cuts else 1.0
    entries = jax.random.normal(rng, extent, jnp.float32) * deviation * loudness
    return jnp.minimum(jnp.maximum(entries, -limit), limit).astype(held_as)


def setup_inputs(seed: int = 0) -> dict:
    arg_keys = jax.random.split(jax.random.key(seed), 4)
    return {
        "logged": draw_logged(jax.random.fold_in(arg_keys[3], 71), 0),
        "fresh": normal_values(arg_keys[1], (M, E), 1.0, 6.0, ((0, 256),)),
        "warm": normal_values(arg_keys[2], (M,), 0.2, 1.0, ((0, 8),), jnp.float32),
    }


EPS = 0.01


def cost_block(block, fresh, fresh_sq):
    wide = block.astype(jnp.float32)
    block_sq = jnp.sum(wide * wide, axis=1)
    inner = jnp.dot(block, fresh.T, preferred_element_type=jnp.float32)
    return (block_sq[:, None] + fresh_sq[None, :] - 2.0 * inner) / E


def reference(logged, fresh, warm):
    fresh_wide = fresh.astype(jnp.float32)
    fresh_sq = jnp.sum(fresh_wide * fresh_wide, axis=1)
    blocks = logged.reshape(N // R_DEV, R_DEV, E)

    def row_pass(block):
        cost = cost_block(block, fresh, fresh_sq)
        expo = (warm[None, :] - cost) / EPS
        top = jnp.max(expo, axis=1)
        total = jnp.sum(jnp.exp(expo - top[:, None]), axis=1)
        return -EPS * (top + jnp.log(total)) - EPS * jnp.log(jnp.float32(N))

    row_potential = lax.map(row_pass, blocks).reshape(N)
    row_blocks = row_potential.reshape(N // R_DEV, R_DEV)

    def col_step(carry, item):
        block, pot = item
        cost = cost_block(block, fresh, fresh_sq)
        expo = (pot[:, None] - cost) / EPS
        top = jnp.max(expo, axis=0)
        total = jnp.sum(jnp.exp(expo - top[None, :]), axis=0)
        old_top, old_total = carry
        both = jnp.maximum(old_top, top)
        merged = old_total * jnp.exp(old_top - both) + total * jnp.exp(top - both)
        return (both, merged), None

    start = (jnp.full((M,), -jnp.inf, jnp.float32), jnp.zeros((M,), jnp.float32))
    (top, total), _ = lax.scan(col_step, start, (blocks, row_blocks))
    col_potential = -EPS * (top + jnp.log(total)) - EPS * jnp.log(jnp.float32(M))

    def reward_pass(item):
        block, pot = item
        cost = cost_block(block, fresh, fresh_sq)
        plan = jnp.exp((pot[:, None] + col_potential[None, :] - cost) / EPS)
        return -jnp.float32(N) * jnp.sum(plan * cost, axis=1)

    reward = lax.map(reward_pass, (blocks, row_blocks)).reshape(N)
    return row_potential, col_potential, reward
```

```python
import functools
import math

import jax
import jax.numpy as jnp
from jax import lax
from jax.experimental import pallas as pl
from jax.experimental.pallas import tpu as pltpu
from jax.sharding import Mesh
from jax.sharding import PartitionSpec as P

EPS = 0.01
AXES = ("zh", "y", "x", "zl", "core")
ROW_GROUP = ("zh", "zl", "core")
COL_GROUP = ("y", "x")
LN2 = math.log(2.0)
LOG2E = 1.0 / LN2


def nt_dot(a, b):
    return lax.dot_general(a, b, (((1,), (1,)), ((), ())), preferred_element_type=jnp.float32)


def lse_kernel(scale, width, x_ref, y_ref, bias_ref, out_ref):
    x = x_ref[...]
    tm = x.shape[0]
    top = None
    total = None
    for start in range(0, y_ref.shape[0], width):
        prod = nt_dot(x, y_ref[start : start + width, :])
        parts = [
            prod[:, o : o + 128] * scale + bias_ref[:, start + o : start + o + 128]
            for o in range(0, width, 128)
        ]
        new = functools.reduce(jnp.maximum, parts)
        if top is not None:
            new = jnp.maximum(new, top)
        add = functools.reduce(jnp.add, [jnp.exp2(p - new) for p in parts])
        total = add if top is None else total * jnp.exp2(top - new) + add
        top = new
    top = top.T
    total = total.T
    best = jnp.max(top, axis=0, keepdims=True)
    out_ref[...] = best + jnp.log2(jnp.sum(total * jnp.exp2(top - best), axis=0, keepdims=True))


def lse(x, y, bias, scale, tm=256, width=1024):
    rows, depth = x.shape
    cols = y.shape[0]
    return pl.pallas_call(
        functools.partial(lse_kernel, scale, width),
        grid=(rows // tm,),
        in_specs=[
            pl.BlockSpec((tm, depth), lambda i: (i, 0)),
            pl.BlockSpec((cols, depth), lambda i: (0, 0)),
            pl.BlockSpec((1, cols), lambda i: (0, 0)),
        ],
        out_specs=pl.BlockSpec((1, tm), lambda i: (0, i)),
        out_shape=jax.ShapeDtypeStruct((1, rows), jnp.float32),
        compiler_params=pltpu.CompilerParams(vmem_limit_bytes=40 * 2**20),
        cost_estimate=pl.CostEstimate(
            flops=2 * rows * cols * depth, bytes_accessed=2 * depth * (rows + cols), transcendentals=rows * cols
        ),
    )(x, y, bias)


def reward_kernel(scale, width, x_ref, y_ref, rbias_ref, rsq_ref, cbias_ref, csq_ref, out_ref):
    x = x_ref[...]
    tm = x.shape[0]
    rbias = jnp.broadcast_to(rbias_ref[...], (128, tm)).T
    mass = jnp.zeros((tm, 128), jnp.float32)
    moment = jnp.zeros((tm, 128), jnp.float32)
    for start in range(0, y_ref.shape[0], width):
        prod = nt_dot(x, y_ref[start : start + width, :])
        for o in range(0, width, 128):
            part = prod[:, o : o + 128]
            cols = slice(start + o, start + o + 128)
            plan = jnp.exp2((part * scale + cbias_ref[:, cols]) + rbias)
            mass = mass + plan
            moment = moment + plan * (part - csq_ref[:, cols])
    mass = jnp.sum(mass.T, axis=0, keepdims=True)
    moment = jnp.sum(moment.T, axis=0, keepdims=True)
    out_ref[...] = rsq_ref[...] * mass - 2.0 * moment


def reward_part(x, y, rbias, rsq, cbias, csq, scale, tm=256, width=1024):
    rows, depth = x.shape
    cols = y.shape[0]
    return pl.pallas_call(
        functools.partial(reward_kernel, scale, width),
        grid=(rows // tm,),
        in_specs=[
            pl.BlockSpec((tm, depth), lambda i: (i, 0)),
            pl.BlockSpec((cols, depth), lambda i: (0, 0)),
            pl.BlockSpec((1, tm), lambda i: (0, i)),
            pl.BlockSpec((1, tm), lambda i: (0, i)),
            pl.BlockSpec((1, cols), lambda i: (0, 0)),
            pl.BlockSpec((1, cols), lambda i: (0, 0)),
        ],
        out_specs=pl.BlockSpec((1, tm), lambda i: (0, i)),
        out_shape=jax.ShapeDtypeStruct((1, rows), jnp.float32),
        compiler_params=pltpu.CompilerParams(vmem_limit_bytes=40 * 2**20),
        cost_estimate=pl.CostEstimate(
            flops=2 * rows * cols * depth, bytes_accessed=2 * depth * (rows + cols), transcendentals=rows * cols
        ),
    )(x, y, rbias, rsq, cbias, csq)


def share(a, axes):
    n = math.prod(lax.axis_size(ax) for ax in axes)
    return lax.all_to_all(jnp.broadcast_to(a[None], (n,) + a.shape), axes, 0, 0)


def merge(parts):
    best = jnp.max(parts, axis=0)
    return best + jnp.log2(jnp.sum(jnp.exp2(parts - best), axis=0))


def body(logged, fresh, warm):
    depth = logged.shape[1]
    zh = lax.axis_index("zh")
    n_rows = logged.shape[0] * 256
    n_cols = fresh.shape[0] * 256

    mine = share(logged, ("zh", "zl"))
    other = lax.ppermute(mine, "core", [(0, 1), (1, 0)])
    core = lax.axis_index("core")
    even = jnp.where(core == 0, mine, other)
    odd = jnp.where(core == 0, other, mine)
    x = jnp.stack([even, odd], axis=1).reshape(-1, depth)
    y = share(fresh, COL_GROUP).reshape(-1, depth)
    rows, cols = x.shape[0], y.shape[0]

    scale = 2.0 * LOG2E / (depth * EPS)
    xw = x.astype(jnp.float32)
    xsq = jnp.sum(xw * xw, axis=1)
    yw = y.astype(jnp.float32)
    ysq = jnp.sum(yw * yw, axis=1)
    warm = lax.dynamic_slice(warm, (zh * cols,), (cols,))

    bias = warm * (LOG2E / EPS) - ysq * (0.5 * scale)
    part = lse(x, y, bias[None], scale)
    total = merge(share(part.reshape(-1), ROW_GROUP))
    rbias = -total - math.log2(n_rows)
    row_all = (rbias + xsq * (0.5 * scale)) * (EPS * LN2)

    part = lse(y, x, rbias[None], scale)
    total = merge(share(part.reshape(-1), COL_GROUP))
    cbias = -total - math.log2(n_cols)
    col_half = (cbias + ysq * (0.5 * scale)) * (EPS * LN2)
    theirs = lax.ppermute(col_half, "zh", [(0, 1), (1, 0)])
    col_potential = jnp.where(
        zh == 0, jnp.concatenate([col_half, theirs]), jnp.concatenate([theirs, col_half])
    )

    part = reward_part(x, y, rbias[None], xsq[None], cbias[None], (0.5 * ysq)[None], scale)
    halves = part.reshape(2, rows // 2)
    sent = jnp.broadcast_to(halves[:, None], (2, 8, rows // 2)).reshape(16, rows // 2)
    got = lax.all_to_all(sent, ROW_GROUP, 0, 0)
    reward = jnp.sum(got, axis=0) * (-n_rows / depth)
    row_potential = lax.dynamic_slice(row_all, (zh * (rows // 2),), (rows // 2,))
    return row_potential, col_potential, reward


def solution(mesh):
    fine = Mesh(mesh.devices.reshape(2, 4, 4, 4, 2), AXES)
    return jax.shard_map(
        body,
        mesh=fine,
        in_specs=(P(AXES, None), P(("zl", "core", "zh", "y", "x"), None), P(("zl", "core"))),
        out_specs=(P(("zh", "y", "x")), P(("zl", "core")), P(("zh", "y", "x"))),
        check_vma=False,
    )
```

```python
import functools
import math

import jax
import jax.numpy as jnp
from jax import lax
from jax.experimental import pallas as pl
from jax.experimental.pallas import tpu as pltpu
from jax.sharding import Mesh
from jax.sharding import PartitionSpec as P

EPS = 0.01
AXES = ("zh", "y", "x", "zl", "core")
ROW_GROUP = ("zh", "zl", "core")
COL_GROUP = ("y", "x")
LN2 = math.log(2.0)
LOG2E = 1.0 / LN2


def nt_dot(a, b):
    return lax.dot_general(a, b, (((1,), (1,)), ((), ())), preferred_element_type=jnp.float32)


SAMPLE = 16

def lse_kernel(scale, width, copies, x_ref, y_ref, bias_ref, few_ref, out_ref):
    tm, cols = x_ref.shape[0], y_ref.shape[0]
    x = x_ref[...]
    step = cols // 16
    few = jnp.concatenate([y_ref[s : s + SAMPLE, :] for s in range(0, cols, step)], axis=0)
    seen = nt_dot(x, few)
    seen = jnp.maximum(seen[:, :128] * scale + few_ref[:, :128], seen[:, 128:] * scale + few_ref[:, 128:])
    base = jnp.max(seen, axis=1, keepdims=True)
    wide = jnp.broadcast_to(base, (tm, 128))
    total = jnp.zeros((tm, 128), jnp.float32)
    for start in range(0, cols, width):
        prod = nt_dot(x, y_ref[start : start + width, :])
        for o in range(0, width, 128):
            total = total + jnp.exp2(
                (prod[:, o : o + 128] * scale + bias_ref[:, start + o : start + o + 128]) - wide
            )
    total = jnp.sum(total, axis=1, keepdims=True)
    value = jnp.broadcast_to(base + jnp.log2(total), (tm, 128)).T
    out_ref[...] = jnp.broadcast_to(value[None, :1], (copies, 1, tm))

    @pl.when(jnp.logical_not(jnp.max(total) < 1e36))
    def _():
        def rows(r, _):
            own = pl.ds(pl.multiple_of(r * 128, 128), 128)
            xs = x_ref[own, :]

            def columns(c, state):
                top, total = state
                at = pl.multiple_of(c * 128, 128)
                part = nt_dot(xs, y_ref[pl.ds(at, 128), :]) * scale + bias_ref[:, pl.ds(at, 128)]
                new = jnp.maximum(top, part)
                return new, total * jnp.exp2(top - new) + jnp.exp2(part - new)

            state = jnp.full((128, 128), -1e38, jnp.float32), jnp.zeros((128, 128), jnp.float32)
            top, total = lax.fori_loop(0, cols // 128, columns, state)
            best = jnp.max(top, axis=1, keepdims=True)
            total = jnp.sum(total * jnp.exp2(top - best), axis=1, keepdims=True)
            value = jnp.broadcast_to(best + jnp.log2(total), (128, 128)).T
            out_ref[:, :, own] = jnp.broadcast_to(value[None, :1], (copies, 1, 128))
            return 0

        lax.fori_loop(0, tm // 128, rows, 0)


def lse(x, y, bias, scale, copies=16, tm=1024, width=256):
    rows, depth = x.shape
    cols = y.shape[0]
    few = bias.reshape(16, cols // 16)[:, :SAMPLE].reshape(1, 16 * SAMPLE)
    return pl.pallas_call(
        functools.partial(lse_kernel, scale, width, copies),
        grid=(rows // tm,),
        in_specs=[
            pl.BlockSpec((tm, depth), lambda i: (i, 0)),
            pl.BlockSpec((cols, depth), lambda i: (0, 0)),
            pl.BlockSpec((1, cols), lambda i: (0, 0)),
            pl.BlockSpec((1, 16 * SAMPLE), lambda i: (0, 0)),
        ],
        out_specs=pl.BlockSpec((copies, 1, tm), lambda i: (0, 0, i)),
        out_shape=jax.ShapeDtypeStruct((copies, 1, rows), jnp.float32),
        compiler_params=pltpu.CompilerParams(vmem_limit_bytes=40 * 2**20),
        cost_estimate=pl.CostEstimate(
            flops=2 * rows * cols * depth, bytes_accessed=2 * depth * (rows + cols), transcendentals=rows * cols
        ),
    )(x, y, bias.reshape(1, cols), few)


def reward_kernel(scale, width, x_ref, y_ref, rbias_ref, rsq_ref, cbias_ref, csq_ref, out_ref):
    x = x_ref[...]
    tm = x.shape[0]
    rbias = jnp.broadcast_to(rbias_ref[...], (128, tm)).T
    mass = jnp.zeros((tm, 128), jnp.float32)
    moment = jnp.zeros((tm, 128), jnp.float32)
    for start in range(0, y_ref.shape[0], width):
        prod = nt_dot(x, y_ref[start : start + width, :])
        for o in range(0, width, 128):
            part = prod[:, o : o + 128]
            cols = slice(start + o, start + o + 128)
            plan = jnp.exp2((part * scale + cbias_ref[:, cols]) + rbias)
            mass = mass + plan
            moment = moment + plan * (part - csq_ref[:, cols])
    mass = jnp.broadcast_to(jnp.sum(mass, axis=1, keepdims=True), (tm, 128)).T[:1]
    moment = jnp.broadcast_to(jnp.sum(moment, axis=1, keepdims=True), (tm, 128)).T[:1]
    half = tm // 2
    value = rsq_ref[...] * mass - 2.0 * moment
    out_ref[:8] = jnp.broadcast_to(value[None, :, :half], (8, 1, half))
    out_ref[8:] = jnp.broadcast_to(value[None, :, half:], (8, 1, half))


def reward_part(x, y, rbias, rsq, cbias, csq, scale, width=256):
    rows, depth = x.shape
    cols = y.shape[0]
    return pl.pallas_call(
        functools.partial(reward_kernel, scale, width),
        out_shape=jax.ShapeDtypeStruct((16, 1, rows // 2), jnp.float32),
        compiler_params=pltpu.CompilerParams(vmem_limit_bytes=40 * 2**20),
        cost_estimate=pl.CostEstimate(
            flops=2 * rows * cols * depth, bytes_accessed=2 * depth * (rows + cols), transcendentals=rows * cols
        ),
    )(x, y, rbias, rsq, cbias, csq)


def copy_kernel(in_ref, out_ref):
    out_ref[...] = in_ref[...][None]


def share(a, axes):
    n = math.prod(lax.axis_size(ax) for ax in axes)
    many = pl.pallas_call(
        copy_kernel,
        grid=(n,),
        in_specs=[pl.BlockSpec(a.shape, lambda i: (0, 0))],
        out_specs=pl.BlockSpec((1,) + a.shape, lambda i: (i, 0, 0)),
        out_shape=jax.ShapeDtypeStruct((n,) + a.shape, a.dtype),
    )(a)
    return lax.all_to_all(many, axes, 0, 0)


def swap(a, axis, bit, before):
    size = lax.axis_size(axis)
    other = lax.ppermute(a, axis, [(i, i ^ bit) for i in range(size)])
    low = (lax.axis_index(axis) & bit) == 0
    return jnp.stack([jnp.where(low, a, other), jnp.where(low, other, a)], axis=before)


def merge(parts):
    parts = parts[:, 0]
    best = jnp.max(parts, axis=0)
    return best + jnp.log2(jnp.sum(jnp.exp2(parts - best), axis=0))


def body(logged, fresh, warm):
    depth = logged.shape[1]
    zh = lax.axis_index("zh")
    n_rows = logged.shape[0] * 256
    n_cols = fresh.shape[0] * 256

    y = share(fresh, COL_GROUP).reshape(-1, depth)
    x = swap(logged, "zh", 1, 0)
    x = swap(x, "zl", 2, 1)
    x = swap(x, "zl", 1, 2)
    x = swap(x, "core", 1, 3).reshape(-1, depth)
    rows, cols = x.shape[0], y.shape[0]

    scale = 2.0 * LOG2E / (depth * EPS)
    xw = x.astype(jnp.float32)
    xsq = jnp.sum(xw * xw, axis=1)
    yw = y.astype(jnp.float32)
    ysq = jnp.sum(yw * yw, axis=1)
    warm = lax.dynamic_slice(warm, (zh * cols,), (cols,))

    bias = warm * (LOG2E / EPS) - ysq * (0.5 * scale)
    part = lse(x, y, bias, scale, tm=rows)
    total = merge(lax.all_to_all(part, ROW_GROUP, 0, 0))
    rbias = -total - math.log2(n_rows)
    row_all = (rbias + xsq * (0.5 * scale)) * (EPS * LN2)

    part = lse(y, x, rbias, scale, tm=cols)
    total = merge(lax.all_to_all(part, COL_GROUP, 0, 0))
    cbias = -total - math.log2(n_cols)
    col_half = (cbias + ysq * (0.5 * scale)) * (EPS * LN2)
    theirs = lax.ppermute(col_half, "zh", [(0, 1), (1, 0)])
    col_potential = jnp.where(
        zh == 0, jnp.concatenate([col_half, theirs]), jnp.concatenate([theirs, col_half])
    )

    part = reward_part(x, y, rbias[None], xsq[None], cbias[None], (0.5 * ysq)[None], scale)
    got = lax.all_to_all(part, ROW_GROUP, 0, 0)
    reward = jnp.sum(got[:, 0], axis=0) * (-n_rows / depth)
    row_potential = lax.dynamic_slice(row_all, (zh * (rows // 2),), (rows // 2,))
    return row_potential, col_potential, reward


def solution(mesh):
    fine = Mesh(mesh.devices.reshape(2, 4, 4, 4, 2), AXES)
    return jax.shard_map(
        body,
        mesh=fine,
        in_specs=(P(AXES, None), P(("zl", "core", "zh", "y", "x"), None), P(("zl", "core"))),
        out_specs=(P(("zh", "y", "x")), P(("zl", "core")), P(("zh", "y", "x"))),
        check_vma=False,
    )
```

```python
import functools
import math

import jax
import jax.numpy as jnp
from jax import lax
from jax.experimental import pallas as pl
from jax.experimental.pallas import tpu as pltpu
from jax.sharding import Mesh
from jax.sharding import PartitionSpec as P

EPS = 0.01
AXES = ("zh", "y", "x", "zl", "core")
ROW_GROUP = ("zh", "zl", "core")
COL_GROUP = ("y", "x")
LN2 = math.log(2.0)
LOG2E = 1.0 / LN2


def nt_dot(a, b):
    return lax.dot_general(a, b, (((1,), (1,)), ((), ())), preferred_element_type=jnp.float32)


SAMPLE = 16
MARGIN = 80.0

def lse_kernel(scale, width, copies, x_ref, y_ref, bias_ref, few_ref, out_ref):
    tm, cols = x_ref.shape[0], y_ref.shape[0]
    x = x_ref[...]
    step = cols // 16
    few = jnp.concatenate([y_ref[s : s + SAMPLE, :] for s in range(0, cols, step)], axis=0)
    seen = nt_dot(x, few)
    seen = jnp.maximum(seen[:, :128] * scale + few_ref[:, :128], seen[:, 128:] * scale + few_ref[:, 128:])
    base = jnp.max(seen, axis=1, keepdims=True) + MARGIN
    wide = jnp.broadcast_to(base, (tm, 128))
    total = jnp.zeros((tm, 128), jnp.float32)
    for start in range(0, cols, width):
        prod = nt_dot(x, y_ref[start : start + width, :])
        for o in range(0, width, 128):
            total = total + jnp.exp2(
                (prod[:, o : o + 128] * scale + bias_ref[:, start + o : start + o + 128]) - wide
            )
    total = jnp.sum(total, axis=1, keepdims=True)
    value = jnp.broadcast_to(base + jnp.log2(total), (tm, 128)).T
    out_ref[...] = jnp.broadcast_to(value[None, :1], (copies, 1, tm))

    @pl.when(jnp.logical_not(jnp.max(total) < 1e36))
    def _():
        def rows(r, _):
            own = pl.ds(pl.multiple_of(r * 128, 128), 128)
            xs = x_ref[own, :]

            def columns(c, state):
                top, total = state
                at = pl.multiple_of(c * 128, 128)
                part = nt_dot(xs, y_ref[pl.ds(at, 128), :]) * scale + bias_ref[:, pl.ds(at, 128)]
                new = jnp.maximum(top, part)
                return new, total * jnp.exp2(top - new) + jnp.exp2(part - new)

            state = jnp.full((128, 128), -1e38, jnp.float32), jnp.zeros((128, 128), jnp.float32)
            top, total = lax.fori_loop(0, cols // 128, columns, state)
            best = jnp.max(top, axis=1, keepdims=True)
            total = jnp.sum(total * jnp.exp2(top - best), axis=1, keepdims=True)
            value = jnp.broadcast_to(best + jnp.log2(total), (128, 128)).T
            out_ref[:, :, own] = jnp.broadcast_to(value[None, :1], (copies, 1, 128))
            return 0

        lax.fori_loop(0, tm // 128, rows, 0)


def lse(x, y, bias, scale, copies=16, tm=1024, width=256):
    rows, depth = x.shape
    cols = y.shape[0]
    few = bias.reshape(16, cols // 16)[:, :SAMPLE].reshape(1, 16 * SAMPLE)
    return pl.pallas_call(
        functools.partial(lse_kernel, scale, width, copies),
        grid=(rows // tm,),
        in_specs=[
            pl.BlockSpec((tm, depth), lambda i: (i, 0)),
            pl.BlockSpec((cols, depth), lambda i: (0, 0)),
            pl.BlockSpec((1, cols), lambda i: (0, 0)),
            pl.BlockSpec((1, 16 * SAMPLE), lambda i: (0, 0)),
        ],
        out_specs=pl.BlockSpec((copies, 1, tm), lambda i: (0, 0, i)),
        out_shape=jax.ShapeDtypeStruct((copies, 1, rows), jnp.float32),
        compiler_params=pltpu.CompilerParams(vmem_limit_bytes=40 * 2**20),
        cost_estimate=pl.CostEstimate(
            flops=2 * rows * cols * depth, bytes_accessed=2 * depth * (rows + cols), transcendentals=rows * cols
        ),
    )(x, y, bias.reshape(1, cols), few)


def reward_kernel(scale, width, x_ref, y_ref, rbias_ref, rsq_ref, cbias_ref, csq_ref, out_ref):
    x = x_ref[...]
    tm = x.shape[0]
    rbias = jnp.broadcast_to(rbias_ref[...], (128, tm)).T
    mass = jnp.zeros((tm, 128), jnp.float32)
    moment = jnp.zeros((tm, 128), jnp.float32)
    for start in range(0, y_ref.shape[0], width):
        prod = nt_dot(x, y_ref[start : start + width, :])
        for o in range(0, width, 128):
            part = prod[:, o : o + 128]
            cols = slice(start + o, start + o + 128)
            plan = jnp.exp2((part * scale + cbias_ref[:, cols]) + rbias)
            mass = mass + plan
            moment = moment + plan * (part - csq_ref[:, cols])
    mass = jnp.broadcast_to(jnp.sum(mass, axis=1, keepdims=True), (tm, 128)).T[:1]
    moment = jnp.broadcast_to(jnp.sum(moment, axis=1, keepdims=True), (tm, 128)).T[:1]
    half = tm // 2
    value = rsq_ref[...] * mass - 2.0 * moment
    out_ref[:8] = jnp.broadcast_to(value[None, :, :half], (8, 1, half))
    out_ref[8:] = jnp.broadcast_to(value[None, :, half:], (8, 1, half))


def reward_part(x, y, rbias, rsq, cbias, csq, scale, width=256):
    rows, depth = x.shape
    cols = y.shape[0]
    return pl.pallas_call(
        functools.partial(reward_kernel, scale, width),
        out_shape=jax.ShapeDtypeStruct((16, 1, rows // 2), jnp.float32),
        compiler_params=pltpu.CompilerParams(vmem_limit_bytes=40 * 2**20),
        cost_estimate=pl.CostEstimate(
            flops=2 * rows * cols * depth, bytes_accessed=2 * depth * (rows + cols), transcendentals=rows * cols
        ),
    )(x, y, rbias, rsq, cbias, csq)


def copy_kernel(in_ref, out_ref):
    out_ref[...] = jnp.broadcast_to(in_ref[...][None], out_ref.shape)


def copies(a, n):
    return pl.pallas_call(copy_kernel, out_shape=jax.ShapeDtypeStruct((n,) + a.shape, a.dtype))(a)


def swap(a, axis, bit, before):
    size = lax.axis_size(axis)
    other = lax.ppermute(a, axis, [(i, i ^ bit) for i in range(size)])
    low = (lax.axis_index(axis) & bit) == 0
    return jnp.stack([jnp.where(low, a, other), jnp.where(low, other, a)], axis=before)


def ring_gather(a, axes):
    n = math.prod(lax.axis_size(ax) for ax in axes)
    me = lax.axis_index(axes)
    zeros = (0,) * a.ndim

    def shift(v, by):
        return lax.ppermute(v, axes, [(i, (i + by) % n) for i in range(n)])

    def put(v, owner):
        return lax.dynamic_update_slice(out, v[None], (lax.rem(owner + n, n),) + zeros)

    out = jnp.zeros((n,) + a.shape, a.dtype)
    out = put(a, me)
    up = down = a
    for s in range(1, n // 2):
        up, down = shift(up, 1), shift(down, -1)
        out = put(up, me - s)
        out = put(down, me + s)
    return put(shift(up, 1), me - n // 2)


def merge(parts):
    parts = parts[:, 0]
    best = jnp.max(parts, axis=0)
    return best + jnp.log2(jnp.sum(jnp.exp2(parts - best), axis=0))


def body(logged, fresh, warm):
    depth = logged.shape[1]
    zh = lax.axis_index("zh")
    n_rows = logged.shape[0] * 256
    n_cols = fresh.shape[0] * 256

    many, logged = lax.optimization_barrier((copies(fresh, 16), logged))
    y = lax.all_to_all(many, COL_GROUP, 0, 0).reshape(-1, depth)
    x = swap(ring_gather(logged, ("zh", "zl")), "core", 1, 1).reshape(-1, depth)
    rows, cols = x.shape[0], y.shape[0]

    scale = 2.0 * LOG2E / (depth * EPS)
    xw = x.astype(jnp.float32)
    xsq = jnp.sum(xw * xw, axis=1)
    yw = y.astype(jnp.float32)
    ysq = jnp.sum(yw * yw, axis=1)
    warm = lax.dynamic_slice(warm, (zh * cols,), (cols,))

    bias = warm * (LOG2E / EPS) - ysq * (0.5 * scale)
    part = lse(x, y, bias, scale, tm=rows)
    total = merge(lax.all_to_all(part, ROW_GROUP, 0, 0))
    rbias = -total - math.log2(n_rows)
    row_all = (rbias + xsq * (0.5 * scale)) * (EPS * LN2)

    part = lse(y, x, rbias, scale, tm=cols)
    total = merge(lax.all_to_all(part, COL_GROUP, 0, 0))
    cbias = -total - math.log2(n_cols)
    col_half = (cbias + ysq * (0.5 * scale)) * (EPS * LN2)
    theirs = lax.ppermute(col_half, "zh", [(0, 1), (1, 0)])
    col_potential = jnp.where(
        zh == 0, jnp.concatenate([col_half, theirs]), jnp.concatenate([theirs, col_half])
    )

    part = reward_part(x, y, rbias[None], xsq[None], cbias[None], (0.5 * ysq)[None], scale)
    got = lax.all_to_all(part, ROW_GROUP, 0, 0)
    reward = jnp.sum(got[:, 0], axis=0) * (-n_rows / depth)
    row_potential = lax.dynamic_slice(row_all, (zh * (rows // 2),), (rows // 2,))
    return row_potential, col_potential, reward


def solution(mesh):
    fine = Mesh(mesh.devices.reshape(2, 4, 4, 4, 2), AXES)
    return jax.shard_map(
        body,
        mesh=fine,
        in_specs=(P(AXES, None), P(("zl", "core", "zh", "y", "x"), None), P(("zl", "core"))),
        out_specs=(P(("zh", "y", "x")), P(("zl", "core")), P(("zh", "y", "x"))),
        check_vma=False,
    )
```

```python
import functools
import math

import jax
import jax.numpy as jnp
from jax import lax
from jax.experimental import pallas as pl
from jax.experimental.pallas import tpu as pltpu
from jax.sharding import Mesh
from jax.sharding import PartitionSpec as P

EPS = 0.01
AXES = ("zh", "y", "x", "zl", "core")
ROW_GROUP = ("zh", "zl", "core")
COL_GROUP = ("y", "x")
LN2 = math.log(2.0)
LOG2E = 1.0 / LN2


def nt_dot(a, b):
    return lax.dot_general(a, b, (((1,), (1,)), ((), ())), preferred_element_type=jnp.float32)


SAMPLE = 16
LARGEST, SMALLEST = 2.0**120, 2.0**-100


def to_row(column, copies=1):
    row = jnp.broadcast_to(column, (column.shape[0], 128)).T[:1]
    return jnp.broadcast_to(row[None], (copies,) + row.shape)


def lse_kernel(scale, blocks, raised, x_ref, y_ref, bias_ref, few_ref, out_ref, moved_ref):
    rows, cols = x_ref.shape[0], y_ref.shape[0]
    copies = out_ref.shape[0]
    step = rows // 16
    some = jnp.concatenate([x_ref[s : s + 2 * SAMPLE, :] for s in range(0, rows, step)], axis=0)
    step = cols // 16
    few = jnp.concatenate([y_ref[s : s + SAMPLE, :] for s in range(0, cols, step)], axis=0)
    seen = nt_dot(some, few) * scale + few_ref[...]
    seen = jnp.maximum(seen[:, :128], seen[:, 128:]).reshape(blocks, -1, 128)
    offset = jnp.max(jnp.max(seen, axis=1), axis=1, keepdims=True) - raised
    moved_ref[...] = bias_ref[...] - offset

    size = rows // blocks
    totals = [jnp.zeros((size, 128), jnp.float32)] * blocks
    for start in range(0, cols, 256):
        prod = nt_dot(x_ref[...], y_ref[start : start + 256, :])
        for b in range(blocks):
            for o in (0, 128):
                part = prod[b * size : (b + 1) * size, o : o + 128]
                at = slice(start + o, start + o + 128)
                totals[b] = totals[b] + jnp.exp2(part * scale + moved_ref[b : b + 1, at])
    safe = None
    for b in range(blocks):
        total = jnp.sum(totals[b], axis=1, keepdims=True)
        value = jnp.log2(total) + offset[b : b + 1, :]
        out_ref[:, :, b * size : (b + 1) * size] = to_row(value, copies)
        good = jnp.logical_and(jnp.min(total) > SMALLEST, jnp.max(total) < LARGEST)
        safe = good if safe is None else jnp.logical_and(safe, good)

    @pl.when(jnp.logical_not(safe))
    def _():
        def some_rows(r, _):
            own = pl.ds(pl.multiple_of(r * 128, 128), 128)
            xs = x_ref[own, :]

            def some_columns(c, state):
                top, total = state
                at = pl.ds(pl.multiple_of(c * 128, 128), 128)
                part = nt_dot(xs, y_ref[at, :]) * scale + bias_ref[:, at]
                new = jnp.maximum(top, part)
                return new, total * jnp.exp2(top - new) + jnp.exp2(part - new)

            state = jnp.full((128, 128), -1e38, jnp.float32), jnp.zeros((128, 128), jnp.float32)
            top, total = lax.fori_loop(0, cols // 128, some_columns, state)
            best = jnp.max(top, axis=1, keepdims=True)
            total = jnp.sum(total * jnp.exp2(top - best), axis=1, keepdims=True)
            out_ref[:, :, own] = to_row(best + jnp.log2(total), copies)
            return 0

        lax.fori_loop(0, rows // 128, some_rows, 0)


def lse(x, y, bias, scale, blocks, raised, copies=16):
    rows, depth = x.shape
    cols = y.shape[0]
    few = bias.reshape(16, cols // 16)[:, :SAMPLE].reshape(1, 16 * SAMPLE)
    return pl.pallas_call(
        functools.partial(lse_kernel, scale, blocks, raised),
        out_shape=jax.ShapeDtypeStruct((copies, 1, rows), jnp.float32),
        scratch_shapes=[pltpu.VMEM((blocks, cols), jnp.float32)],
        compiler_params=pltpu.CompilerParams(vmem_limit_bytes=40 * 2**20),
        cost_estimate=pl.CostEstimate(
            flops=2 * rows * cols * depth, bytes_accessed=2 * depth * (rows + cols), transcendentals=rows * cols
        ),
    )(x, y, bias.reshape(1, cols), few)


SPREAD = 150.0
SHIFT = 100.0


def reward_kernel(scale, x_ref, y_ref, rbias_ref, rsq_ref, cbias_ref, csq_ref, out_ref):
    rows, cols = x_ref.shape[0], y_ref.shape[0]
    least = jnp.min(rbias_ref[...])
    near = jnp.max(rbias_ref[...]) - least <= SPREAD
    shift = least + SHIFT

    def report(value):
        half = rows // 2
        out_ref[:8] = jnp.broadcast_to(value[None, :, :half], (8, 1, half))
        out_ref[8:] = jnp.broadcast_to(value[None, :, half:], (8, 1, half))

    @pl.when(near)
    def _():
        mass = jnp.zeros((rows, 128), jnp.float32)
        moment = jnp.zeros((rows, 128), jnp.float32)
        for start in range(0, cols, 256):
            prod = nt_dot(x_ref[...], y_ref[start : start + 256, :])
            for o in (0, 128):
                part = prod[:, o : o + 128]
                at = slice(start + o, start + o + 128)
                plan = jnp.exp2(part * scale + (cbias_ref[:, at] + shift))
                mass = mass + plan
                moment = moment + plan * (part - csq_ref[:, at])
        mass = to_row(jnp.sum(mass, axis=1, keepdims=True))[0]
        moment = to_row(jnp.sum(moment, axis=1, keepdims=True))[0]
        report(jnp.exp2(rbias_ref[...] - shift) * (rsq_ref[...] * mass - 2.0 * moment))

    @pl.when(jnp.logical_not(near))
    def _():
        def some_rows(r, value):
            own = pl.ds(pl.multiple_of(r * 128, 128), 128)
            xs = x_ref[own, :]
            rbias = jnp.broadcast_to(rbias_ref[:, own], (128, 128)).T

            def some_columns(c, state):
                mass, moment = state
                at = pl.ds(pl.multiple_of(c * 128, 128), 128)
                part = nt_dot(xs, y_ref[at, :])
                plan = jnp.exp2((part * scale + cbias_ref[:, at]) + rbias)
                return mass + plan, moment + plan * (part - csq_ref[:, at])

            state = jnp.zeros((128, 128), jnp.float32), jnp.zeros((128, 128), jnp.float32)
            mass, moment = lax.fori_loop(0, cols // 128, some_columns, state)
            mass = to_row(jnp.sum(mass, axis=1, keepdims=True))
            moment = to_row(jnp.sum(moment, axis=1, keepdims=True))
            value = rsq_ref[:, own][None] * mass - 2.0 * moment
            half = rows // 256

            @pl.when(r < half)
            def _():
                out_ref[:8, :, own] = jnp.broadcast_to(value, (8, 1, 128))

            @pl.when(r >= half)
            def _():
                there = pl.ds(pl.multiple_of((r - half) * 128, 128), 128)
                out_ref[8:, :, there] = jnp.broadcast_to(value, (8, 1, 128))

            return 0

        lax.fori_loop(0, rows // 128, some_rows, 0)


def reward_part(x, y, rbias, rsq, cbias, csq, scale):
    rows, depth = x.shape
    cols = y.shape[0]
    return pl.pallas_call(
        functools.partial(reward_kernel, scale),
        out_shape=jax.ShapeDtypeStruct((16, 1, rows // 2), jnp.float32),
        compiler_params=pltpu.CompilerParams(vmem_limit_bytes=40 * 2**20),
        cost_estimate=pl.CostEstimate(
            flops=2 * rows * cols * depth, bytes_accessed=2 * depth * (rows + cols), transcendentals=rows * cols
        ),
    )(x, y, rbias, rsq, cbias, csq)


def copy_kernel(in_ref, out_ref):
    out_ref[...] = jnp.broadcast_to(in_ref[...][None], out_ref.shape)


def copies(a, n):
    return pl.pallas_call(copy_kernel, out_shape=jax.ShapeDtypeStruct((n,) + a.shape, a.dtype))(a)


def swap(a, axis, bit, before):
    size = lax.axis_size(axis)
    other = lax.ppermute(a, axis, [(i, i ^ bit) for i in range(size)])
    low = (lax.axis_index(axis) & bit) == 0
    return jnp.stack([jnp.where(low, a, other), jnp.where(low, other, a)], axis=before)


def ring_gather(a, axes):
    n = math.prod(lax.axis_size(ax) for ax in axes)
    me = lax.axis_index(axes)
    zeros = (0,) * a.ndim

    def shift(v, by):
        return lax.ppermute(v, axes, [(i, (i + by) % n) for i in range(n)])

    def put(v, owner):
        return lax.dynamic_update_slice(out, v[None], (lax.rem(owner + n, n),) + zeros)

    out = jnp.zeros((n,) + a.shape, a.dtype)
    out = put(a, me)
    up = down = a
    for s in range(1, n // 2):
        up, down = shift(up, 1), shift(down, -1)
        out = put(up, me - s)
        out = put(down, me + s)
    return put(shift(up, 1), me - n // 2)


def merge(parts):
    parts = parts[:, 0]
    best = jnp.max(parts, axis=0)
    return best + jnp.log2(jnp.sum(jnp.exp2(parts - best), axis=0))


def body(logged, fresh, warm):
    depth = logged.shape[1]
    zh = lax.axis_index("zh")
    n_rows = logged.shape[0] * 256
    n_cols = fresh.shape[0] * 256

    many, logged = lax.optimization_barrier((copies(fresh, 16), logged))
    y = lax.all_to_all(many, COL_GROUP, 0, 0).reshape(-1, depth)
    x = swap(ring_gather(logged, ("zh", "zl")), "core", 1, 1).reshape(-1, depth)
    rows, cols = x.shape[0], y.shape[0]

    scale = 2.0 * LOG2E / (depth * EPS)
    xw = x.astype(jnp.float32)
    xsq = jnp.sum(xw * xw, axis=1)
    yw = y.astype(jnp.float32)
    ysq = jnp.sum(yw * yw, axis=1)
    warm = lax.dynamic_slice(warm, (zh * cols,), (cols,))

    bias = warm * (LOG2E / EPS) - ysq * (0.5 * scale)
    part = lse(x, y, bias, scale, 1, 0.0)
    total = merge(lax.all_to_all(part, ROW_GROUP, 0, 0))
    rbias = -total - math.log2(n_rows)
    row_all = (rbias + xsq * (0.5 * scale)) * (EPS * LN2)

    part = lse(y, x, rbias, scale, 16, 14.0)
    total = merge(lax.all_to_all(part, COL_GROUP, 0, 0))
    cbias = -total - math.log2(n_cols)
    col_half = (cbias + ysq * (0.5 * scale)) * (EPS * LN2)
    theirs = lax.ppermute(col_half, "zh", [(0, 1), (1, 0)])
    col_potential = jnp.where(
        zh == 0, jnp.concatenate([col_half, theirs]), jnp.concatenate([theirs, col_half])
    )

    part = reward_part(x, y, rbias[None], xsq[None], cbias[None], (0.5 * ysq)[None], scale)
    part, col_potential = lax.optimization_barrier((part, col_potential))
    got = lax.all_to_all(part, ROW_GROUP, 0, 0)
    reward = jnp.sum(got[:, 0], axis=0) * (-n_rows / depth)
    row_potential = lax.dynamic_slice(row_all, (zh * (rows // 2),), (rows // 2,))
    return row_potential, col_potential, reward


def solution(mesh):
    fine = Mesh(mesh.devices.reshape(2, 4, 4, 4, 2), AXES)
    return jax.shard_map(
        body,
        mesh=fine,
        in_specs=(P(AXES, None), P(("zl", "core", "zh", "y", "x"), None), P(("zl", "core"))),
        out_specs=(P(("zh", "y", "x")), P(("zl", "core")), P(("zh", "y", "x"))),
        check_vma=False,
    )
```

```python
import functools
import math

import jax
import jax.numpy as jnp
from jax import lax
from jax.experimental import pallas as pl
from jax.experimental.pallas import tpu as pltpu
from jax.sharding import Mesh
from jax.sharding import PartitionSpec as P

EPS = 0.01
AXES = ("zh", "y", "x", "zl", "core")
ROW_GROUP = ("zh", "zl", "core")
COL_GROUP = ("y", "x")
LN2 = math.log(2.0)
LOG2E = 1.0 / LN2


def nt_dot(a, b):
    return lax.dot_general(a, b, (((1,), (1,)), ((), ())), preferred_element_type=jnp.float32)


SAMPLE = 16
LARGEST, SMALLEST = 2.0**110, 2.0**-100


def to_row(column, copies=1):
    row = jnp.broadcast_to(column, (column.shape[0], 128)).T[:1]
    return jnp.broadcast_to(row[None], (copies,) + row.shape)


def lse_kernel(scale, blocks, raised, x_ref, y_ref, bias_ref, few_ref, out_ref, moved_ref):
    rows, cols = x_ref.shape[0], y_ref.shape[0]
    copies = out_ref.shape[0]
    step = rows // 16
    some = jnp.concatenate([x_ref[s : s + 2 * SAMPLE, :] for s in range(0, rows, step)], axis=0)
    step = cols // 16
    few = jnp.concatenate([y_ref[s : s + SAMPLE, :] for s in range(0, cols, step)], axis=0)
    seen = nt_dot(some, few) * scale + few_ref[...]
    seen = jnp.maximum(seen[:, :128], seen[:, 128:]).reshape(blocks, -1, 128)
    offset = jnp.max(jnp.max(seen, axis=1), axis=1, keepdims=True) - raised
    moved_ref[...] = bias_ref[...] - offset

    size = rows // blocks
    totals = [jnp.zeros((size, 128), jnp.float32)] * blocks
    for start in range(0, cols, 256):
        prod = nt_dot(x_ref[...], y_ref[start : start + 256, :])
        for b in range(blocks):
            for o in (0, 128):
                part = prod[b * size : (b + 1) * size, o : o + 128]
                at = slice(start + o, start + o + 128)
                totals[b] = totals[b] + jnp.exp2(part * scale + moved_ref[b : b + 1, at])
    safe = None
    for b in range(blocks):
        total = jnp.sum(totals[b], axis=1, keepdims=True)
        value = jnp.log2(total) + offset[b : b + 1, :]
        out_ref[:, :, b * size : (b + 1) * size] = to_row(value, copies)
        good = jnp.logical_and(jnp.min(total) > SMALLEST, jnp.max(total) < LARGEST)
        safe = good if safe is None else jnp.logical_and(safe, good)

    @pl.when(jnp.logical_not(safe))
    def _():
        def some_rows(r, _):
            own = pl.ds(pl.multiple_of(r * 128, 128), 128)
            xs = x_ref[own, :]

            def some_columns(c, state):
                top, total = state
                at = pl.ds(pl.multiple_of(c * 128, 128), 128)
                part = nt_dot(xs, y_ref[at, :]) * scale + bias_ref[:, at]
                new = jnp.maximum(top, part)
                return new, total * jnp.exp2(top - new) + jnp.exp2(part - new)

            state = jnp.full((128, 128), -1e38, jnp.float32), jnp.zeros((128, 128), jnp.float32)
            top, total = lax.fori_loop(0, cols // 128, some_columns, state)
            best = jnp.max(top, axis=1, keepdims=True)
            total = jnp.sum(total * jnp.exp2(top - best), axis=1, keepdims=True)
            out_ref[:, :, own] = to_row(best + jnp.log2(total), copies)
            return 0

        lax.fori_loop(0, rows // 128, some_rows, 0)


def lse(x, y, bias, scale, blocks, raised, copies=16):
    rows, depth = x.shape
    cols = y.shape[0]
    few = bias.reshape(16, cols // 16)[:, :SAMPLE].reshape(1, 16 * SAMPLE)
    return pl.pallas_call(
        functools.partial(lse_kernel, scale, blocks, raised),
        out_shape=jax.ShapeDtypeStruct((copies, 1, rows), jnp.float32),
        scratch_shapes=[pltpu.VMEM((blocks, cols), jnp.float32)],
        compiler_params=pltpu.CompilerParams(vmem_limit_bytes=40 * 2**20),
        cost_estimate=pl.CostEstimate(
            flops=2 * rows * cols * depth, bytes_accessed=2 * depth * (rows + cols), transcendentals=rows * cols
        ),
    )(x, y, bias.reshape(1, cols), few)


def over_lanes(row):
    high = row.astype(jnp.bfloat16)
    rest = row - high.astype(jnp.float32)
    mid = rest.astype(jnp.bfloat16)
    low = (rest - mid.astype(jnp.float32)).astype(jnp.bfloat16)
    parts = jnp.concatenate([high, mid, low, jnp.zeros((13, row.shape[1]), jnp.bfloat16)], axis=0)
    ones = jnp.ones((16, 128), jnp.bfloat16)
    return lax.dot_general(parts, ones, (((0,), (0,)), ((), ())), preferred_element_type=jnp.float32)


def fold(a, height):
    return jnp.sum(a.reshape(a.shape[0] // height, height, a.shape[1]), axis=0)


MB = 512
HEADROOM = 40.0
HEADROOM_LIMIT = -160.0


def column_kernel(scale, raised, x_ref, y_ref, rbias_ref, rsq_ref, csq_ref, out_ref, low_ref, high_ref, info_ref, wide_ref, pot_ref):
    rows, cols = x_ref.shape[0], y_ref.shape[0]
    copies = out_ref.shape[0]
    wide_ref[...] = over_lanes(rbias_ref[...])
    step = cols // 16
    some = jnp.concatenate([y_ref[s : s + 2 * SAMPLE, :] for s in range(0, cols, step)], axis=0)
    step = rows // 16
    few = jnp.concatenate([x_ref[s : s + SAMPLE, :] for s in range(0, rows, step)], axis=0)
    few_bias = jnp.concatenate([wide_ref[s : s + SAMPLE, :] for s in range(0, rows, step)], axis=0)
    seen = nt_dot(few, some)
    seen = functools.reduce(jnp.maximum, [seen[:, o : o + 128] * scale + few_bias for o in range(0, 512, 128)])
    offset = jnp.max(jnp.max(seen, axis=0, keepdims=True), axis=1, keepdims=True) - raised
    wide_ref[...] = wide_ref[...] - offset
    pot_ref[...] = over_lanes(rbias_ref[...] + (0.5 * scale) * rsq_ref[...] - offset)

    smallest = largest = None
    for t in range(0, cols, 256):
        totals = [jnp.zeros((32, 128), jnp.float32)] * 2
        for start in range(0, rows, MB):
            prod = nt_dot(x_ref[start : start + MB, :], y_ref[t : t + 256, :])
            wide = wide_ref[start : start + MB, :]
            pot = pot_ref[start : start + MB, :]
            for b in (0, 1):
                at = slice(t + b * 128, t + b * 128 + 128)
                power = prod[:, b * 128 : b * 128 + 128] * scale + wide
                term = jnp.exp2(power)
                totals[b] = totals[b] + fold(term, 32)
                terms_ref = low_ref if start < rows // 2 else high_ref
                place = start % (rows // 2)
                terms_ref[place : place + MB, at] = term * ((scale * csq_ref[:, at] - power) + pot)
        for b in (0, 1):
            total = jnp.sum(totals[b], axis=0, keepdims=True)
            smallest = total if smallest is None else jnp.minimum(smallest, total)
            largest = total if largest is None else jnp.maximum(largest, total)
            at = slice(t + b * 128, t + b * 128 + 128)
            out_ref[:, :, at] = jnp.broadcast_to((jnp.log2(total) + offset)[None], (copies, 1, 128))
    safe = jnp.logical_and(jnp.min(smallest) > SMALLEST, jnp.max(largest) < LARGEST)
    info_ref[:1, :] = jnp.broadcast_to(offset, (1, 128))
    info_ref[1:, :] = jnp.broadcast_to(jnp.where(safe, 1.0, 0.0), (1, 128))

    @pl.when(jnp.logical_not(safe))
    def _():
        def some_columns(c, _):
            own = pl.ds(pl.multiple_of(c * 128, 128), 128)
            ys = y_ref[own, :]

            def some_rows(r, state):
                top, total = state
                at = pl.ds(pl.multiple_of(r * 128, 128), 128)
                part = nt_dot(ys, x_ref[at, :]) * scale + rbias_ref[:, at]
                new = jnp.maximum(top, part)
                return new, total * jnp.exp2(top - new) + jnp.exp2(part - new)

            state = jnp.full((128, 128), -1e38, jnp.float32), jnp.zeros((128, 128), jnp.float32)
            top, total = lax.fori_loop(0, rows // 128, some_rows, state)
            best = jnp.max(top, axis=1, keepdims=True)
            total = jnp.sum(total * jnp.exp2(top - best), axis=1, keepdims=True)
            out_ref[:, :, own] = to_row(best + jnp.log2(total), copies)
            return 0

        lax.fori_loop(0, cols // 128, some_columns, 0)


def column_part(x, y, rbias, rsq, csq, scale, raised, copies=16):
    rows, depth = x.shape
    cols = y.shape[0]
    vmem = pl.BlockSpec(memory_space=pltpu.VMEM)
    return pl.pallas_call(
        functools.partial(column_kernel, scale, raised),
        in_specs=[vmem] * 5,
        out_specs=[vmem] * 4,
        out_shape=[
            jax.ShapeDtypeStruct((copies, 1, cols), jnp.float32),
            jax.ShapeDtypeStruct((rows // 2, cols), jnp.float32),
            jax.ShapeDtypeStruct((rows // 2, cols), jnp.float32),
            jax.ShapeDtypeStruct((2, 128), jnp.float32),
        ],
        scratch_shapes=[pltpu.VMEM((rows, 128), jnp.float32)] * 2,
        compiler_params=pltpu.CompilerParams(vmem_limit_bytes=8 * 2**20),
        cost_estimate=pl.CostEstimate(
            flops=2 * rows * cols * depth, bytes_accessed=2 * depth * (rows + cols), transcendentals=rows * cols
        ),
    )(x, y, rbias, rsq, csq)


def reward_kernel(
    scale, factor, n_cols, parts_ref, x_ref, y_ref, rbias_ref, rsq_ref, csq_ref, low_ref, high_ref, info_ref, out_ref, pot_ref, cbias_ref
):
    rows, cols = x_ref.shape[0], y_ref.shape[0]
    half = rows // 2
    best = functools.reduce(jnp.maximum, [parts_ref[i] for i in range(parts_ref.shape[0])])
    total = functools.reduce(jnp.add, [jnp.exp2(parts_ref[i] - best) for i in range(parts_ref.shape[0])])
    cbias_ref[...] = -(best + jnp.log2(total)) - math.log2(n_cols)
    pot_ref[...] = (cbias_ref[...] + scale * csq_ref[...]) * (EPS * LN2)
    offset = jnp.max(info_ref[:1, :])
    far = jnp.min(cbias_ref[...]) + offset < HEADROOM_LIMIT
    usable = jnp.logical_and(jnp.min(info_ref[1:, :]) > 0.5, jnp.logical_not(far))

    @pl.when(usable)
    def _():
        gain = jnp.exp2(cbias_ref[...] + (offset + HEADROOM))
        for r in range(0, rows, 128):
            terms_ref, first, place = (low_ref, 0, r) if r < half else (high_ref, 8, r - half)
            total = jnp.zeros((128, 128), jnp.float32)
            for o in range(0, cols, 128):
                total = total + terms_ref[place : place + 128, o : o + 128] * gain[:, o : o + 128]
            value = to_row(jnp.sum(total, axis=1, keepdims=True), 8) * (factor * 2.0 ** (1.0 - HEADROOM) / scale)
            out_ref[first : first + 8, :, place : place + 128] = value

    @pl.when(jnp.logical_not(usable))
    def _():
        def some_rows(r, _):
            own = pl.ds(pl.multiple_of(r * 128, 128), 128)
            xs = x_ref[own, :]
            rbias = jnp.broadcast_to(rbias_ref[:, own], (128, 128)).T

            def some_columns(c, state):
                mass, moment = state
                at = pl.ds(pl.multiple_of(c * 128, 128), 128)
                part = nt_dot(xs, y_ref[at, :])
                plan = jnp.exp2((part * scale + cbias_ref[:, at]) + rbias)
                return mass + plan, moment + plan * (part - csq_ref[:, at])

            state = jnp.zeros((128, 128), jnp.float32), jnp.zeros((128, 128), jnp.float32)
            mass, moment = lax.fori_loop(0, cols // 128, some_columns, state)
            mass = to_row(jnp.sum(mass, axis=1, keepdims=True))
            moment = to_row(jnp.sum(moment, axis=1, keepdims=True))
            value = factor * (rsq_ref[:, own][None] * mass - 2.0 * moment)

            @pl.when(r < half // 128)
            def _():
                out_ref[:8, :, own] = jnp.broadcast_to(value, (8, 1, 128))

            @pl.when(r >= half // 128)
            def _():
                there = pl.ds(pl.multiple_of(r * 128 - half, 128), 128)
                out_ref[8:, :, there] = jnp.broadcast_to(value, (8, 1, 128))

            return 0

        lax.fori_loop(0, rows // 128, some_rows, 0)


def reward_part(parts, x, y, rbias, rsq, csq, low, high, info, scale, factor, n_cols):
    rows, cols = x.shape[0], y.shape[0]
    vmem = pl.BlockSpec(memory_space=pltpu.VMEM)
    return pl.pallas_call(
        functools.partial(reward_kernel, scale, factor, n_cols),
        in_specs=[vmem] * 9,
        out_specs=[vmem] * 2,
        out_shape=[
            jax.ShapeDtypeStruct((16, 1, rows // 2), jnp.float32),
            jax.ShapeDtypeStruct((1, cols), jnp.float32),
        ],
        scratch_shapes=[pltpu.VMEM((1, cols), jnp.float32)],
        compiler_params=pltpu.CompilerParams(vmem_limit_bytes=8 * 2**20),
        cost_estimate=pl.CostEstimate(flops=2 * rows * cols, bytes_accessed=4 * rows * cols, transcendentals=0),
    )(parts, x, y, rbias, rsq, csq, low, high, info)


def copy_kernel(in_ref, out_ref):
    out_ref[...] = jnp.broadcast_to(in_ref[...][None], out_ref.shape)


def copies(a, n):
    return pl.pallas_call(copy_kernel, out_shape=jax.ShapeDtypeStruct((n,) + a.shape, a.dtype))(a)


def swap(a, axis, bit, before):
    size = lax.axis_size(axis)
    other = lax.ppermute(a, axis, [(i, i ^ bit) for i in range(size)])
    low = (lax.axis_index(axis) & bit) == 0
    return jnp.stack([jnp.where(low, a, other), jnp.where(low, other, a)], axis=before)


def ring_gather(a, axes):
    n = math.prod(lax.axis_size(ax) for ax in axes)
    me = lax.axis_index(axes)
    zeros = (0,) * a.ndim

    def shift(v, by):
        return lax.ppermute(v, axes, [(i, (i + by) % n) for i in range(n)])

    def put(v, owner):
        return lax.dynamic_update_slice(out, v[None], (lax.rem(owner + n, n),) + zeros)

    out = jnp.zeros((n,) + a.shape, a.dtype)
    out = put(a, me)
    up = down = a
    for s in range(1, n // 2):
        up, down = shift(up, 1), shift(down, -1)
        out = put(up, me - s)
        out = put(down, me + s)
    return put(shift(up, 1), me - n // 2)


def merge(parts):
    parts = parts[:, 0]
    best = jnp.max(parts, axis=0)
    return best + jnp.log2(jnp.sum(jnp.exp2(parts - best), axis=0))


def body(logged, fresh, warm):
    depth = logged.shape[1]
    first = lax.axis_index("zh") == 0
    n_rows = logged.shape[0] * 256
    n_cols = fresh.shape[0] * 256

    many, logged, first = lax.optimization_barrier((copies(fresh, 16), logged, first))
    y = lax.all_to_all(many, COL_GROUP, 0, 0).reshape(-1, depth)
    x = swap(ring_gather(logged, ("zh", "zl")), "core", 1, 1).reshape(-1, depth)
    rows, cols = x.shape[0], y.shape[0]

    scale = 2.0 * LOG2E / (depth * EPS)
    xw = x.astype(jnp.float32)
    xsq = jnp.sum(xw * xw, axis=1)
    yw = y.astype(jnp.float32)
    ysq = jnp.sum(yw * yw, axis=1)
    warm = jnp.where(first, warm[:cols], warm[cols:])

    bias = warm * (LOG2E / EPS) - ysq * (0.5 * scale)
    part = lse(x, y, bias, scale, 1, 0.0)
    total = merge(lax.all_to_all(part, ROW_GROUP, 0, 0))
    rbias = -total - math.log2(n_rows)
    row_all = (rbias + xsq * (0.5 * scale)) * (EPS * LN2)

    part, low, high, info = column_part(x, y, rbias[None], xsq[None], (0.5 * ysq)[None], scale, 30.0)
    parts = lax.all_to_all(part, COL_GROUP, 0, 0)
    part, col_half = reward_part(
        parts, x, y, rbias[None], xsq[None], (0.5 * ysq)[None], low, high, info, scale, -n_rows / depth, n_cols
    )
    got = lax.all_to_all(part, ROW_GROUP, 0, 0)
    reward = jnp.sum(got[:, 0], axis=0)
    theirs = lax.ppermute(col_half, "zh", [(0, 1), (1, 0)])
    mine, theirs = col_half[0], theirs[0]
    col_potential = jnp.where(first, jnp.concatenate([mine, theirs]), jnp.concatenate([theirs, mine]))
    row_potential = jnp.where(first, row_all[: rows // 2], row_all[rows // 2 :])
    return row_potential, col_potential, reward


def solution(mesh):
    fine = Mesh(mesh.devices.reshape(2, 4, 4, 4, 2), AXES)
    return jax.shard_map(
        body,
        mesh=fine,
        in_specs=(P(AXES, None), P(("zl", "core", "zh", "y", "x"), None), P(("zl", "core"))),
        out_specs=(P(("zh", "y", "x")), P(("zl", "core")), P(("zh", "y", "x"))),
        check_vma=False,
    )
```

```python
import functools
import math

import jax
import jax.numpy as jnp
from jax import lax
from jax.experimental import pallas as pl
from jax.experimental.pallas import tpu as pltpu
from jax.sharding import Mesh
from jax.sharding import PartitionSpec as P

EPS = 0.01
AXES = ("zh", "y", "x", "zl", "core")
ROW_GROUP = ("zh", "core", "zl")
COL_GROUP = ("x", "y")
LN2 = math.log(2.0)
LOG2E = 1.0 / LN2


def nt_dot(a, b):
    return lax.dot_general(a, b, (((1,), (1,)), ((), ())), preferred_element_type=jnp.float32)


SAMPLE = 16
LARGEST, SMALLEST = 2.0**110, 2.0**-100


def to_row(column, copies=1):
    row = jnp.broadcast_to(column, (column.shape[0], 128)).T[:1]
    return jnp.broadcast_to(row[None], (copies,) + row.shape)


def lse_kernel(scale, blocks, raised, x_ref, y_ref, bias_ref, few_ref, out_ref, moved_ref):
    rows, cols = x_ref.shape[0], y_ref.shape[0]
    copies = out_ref.shape[0]
    step = rows // 16
    some = jnp.concatenate([x_ref[s : s + 2 * SAMPLE, :] for s in range(0, rows, step)], axis=0)
    step = cols // 16
    few = jnp.concatenate([y_ref[s : s + SAMPLE, :] for s in range(0, cols, step)], axis=0)
    seen = nt_dot(some, few) * scale + few_ref[...]
    seen = jnp.maximum(seen[:, :128], seen[:, 128:]).reshape(blocks, -1, 128)
    offset = jnp.max(jnp.max(seen, axis=1), axis=1, keepdims=True) - raised
    moved_ref[...] = bias_ref[...] - offset

    size = rows // blocks
    totals = [jnp.zeros((size, 128), jnp.float32)] * blocks
    for start in range(0, cols, 256):
        prod = nt_dot(x_ref[...], y_ref[start : start + 256, :])
        for b in range(blocks):
            for o in (0, 128):
                part = prod[b * size : (b + 1) * size, o : o + 128]
                at = slice(start + o, start + o + 128)
                totals[b] = totals[b] + jnp.exp2(part * scale + moved_ref[b : b + 1, at])
    safe = None
    for b in range(blocks):
        total = jnp.sum(totals[b], axis=1, keepdims=True)
        value = jnp.log2(total) + offset[b : b + 1, :]
        out_ref[:, :, b * size : (b + 1) * size] = to_row(value, copies)
        good = jnp.logical_and(jnp.min(total) > SMALLEST, jnp.max(total) < LARGEST)
        safe = good if safe is None else jnp.logical_and(safe, good)

    @pl.when(jnp.logical_not(safe))
    def _():
        def some_rows(r, _):
            own = pl.ds(pl.multiple_of(r * 128, 128), 128)
            xs = x_ref[own, :]

            def some_columns(c, state):
                top, total = state
                at = pl.ds(pl.multiple_of(c * 128, 128), 128)
                part = nt_dot(xs, y_ref[at, :]) * scale + bias_ref[:, at]
                new = jnp.maximum(top, part)
                return new, total * jnp.exp2(top - new) + jnp.exp2(part - new)

            state = jnp.full((128, 128), -1e38, jnp.float32), jnp.zeros((128, 128), jnp.float32)
            top, total = lax.fori_loop(0, cols // 128, some_columns, state)
            best = jnp.max(top, axis=1, keepdims=True)
            total = jnp.sum(total * jnp.exp2(top - best), axis=1, keepdims=True)
            out_ref[:, :, own] = to_row(best + jnp.log2(total), copies)
            return 0

        lax.fori_loop(0, rows // 128, some_rows, 0)


def lse(x, y, bias, scale, blocks, raised, copies=16):
    rows, depth = x.shape
    cols = y.shape[0]
    few = bias.reshape(16, cols // 16)[:, :SAMPLE].reshape(1, 16 * SAMPLE)
    return pl.pallas_call(
        functools.partial(lse_kernel, scale, blocks, raised),
        out_shape=jax.ShapeDtypeStruct((copies, 1, rows), jnp.float32),
        scratch_shapes=[pltpu.VMEM((blocks, cols), jnp.float32)],
        compiler_params=pltpu.CompilerParams(vmem_limit_bytes=40 * 2**20),
        cost_estimate=pl.CostEstimate(
            flops=2 * rows * cols * depth, bytes_accessed=2 * depth * (rows + cols), transcendentals=rows * cols
        ),
    )(x, y, bias.reshape(1, cols), few)


def over_lanes(row):
    high = row.astype(jnp.bfloat16)
    rest = row - high.astype(jnp.float32)
    mid = rest.astype(jnp.bfloat16)
    low = (rest - mid.astype(jnp.float32)).astype(jnp.bfloat16)
    parts = jnp.concatenate([high, mid, low, jnp.zeros((13, row.shape[1]), jnp.bfloat16)], axis=0)
    ones = jnp.ones((16, 128), jnp.bfloat16)
    return lax.dot_general(parts, ones, (((0,), (0,)), ((), ())), preferred_element_type=jnp.float32)


def fold(a, height):
    return jnp.sum(a.reshape(a.shape[0] // height, height, a.shape[1]), axis=0)


MB = 512
HEADROOM = 40.0
HEADROOM_LIMIT = -160.0


def column_kernel(scale, raised, x_ref, y_ref, rbias_ref, rsq_ref, csq_ref, out_ref, low_ref, high_ref, info_ref, wide_ref, pot_ref):
    rows, cols = x_ref.shape[0], y_ref.shape[0]
    copies = out_ref.shape[0]
    wide_ref[...] = over_lanes(rbias_ref[...])
    step = cols // 16
    some = jnp.concatenate([y_ref[s : s + 2 * SAMPLE, :] for s in range(0, cols, step)], axis=0)
    step = rows // 16
    few = jnp.concatenate([x_ref[s : s + SAMPLE, :] for s in range(0, rows, step)], axis=0)
    few_bias = jnp.concatenate([wide_ref[s : s + SAMPLE, :] for s in range(0, rows, step)], axis=0)
    seen = nt_dot(few, some)
    seen = functools.reduce(jnp.maximum, [seen[:, o : o + 128] * scale + few_bias for o in range(0, 512, 128)])
    offset = jnp.max(jnp.max(seen, axis=0, keepdims=True), axis=1, keepdims=True) - raised
    wide_ref[...] = wide_ref[...] - offset
    pot_ref[...] = over_lanes(rbias_ref[...] + (0.5 * scale) * rsq_ref[...] - offset)

    smallest = largest = None
    for t in range(0, cols, 256):
        totals = [jnp.zeros((32, 128), jnp.float32)] * 2
        for start in range(0, rows, MB):
            prod = nt_dot(x_ref[start : start + MB, :], y_ref[t : t + 256, :])
            wide = wide_ref[start : start + MB, :]
            pot = pot_ref[start : start + MB, :]
            for b in (0, 1):
                at = slice(t + b * 128, t + b * 128 + 128)
                power = prod[:, b * 128 : b * 128 + 128] * scale + wide
                term = jnp.exp2(power)
                totals[b] = totals[b] + fold(term, 32)
                terms_ref = low_ref if start < rows // 2 else high_ref
                place = start % (rows // 2)
                terms_ref[place : place + MB, at] = term * ((scale * csq_ref[:, at] - power) + pot)
        for b in (0, 1):
            total = jnp.sum(totals[b], axis=0, keepdims=True)
            smallest = total if smallest is None else jnp.minimum(smallest, total)
            largest = total if largest is None else jnp.maximum(largest, total)
            at = slice(t + b * 128, t + b * 128 + 128)
            out_ref[:, :, at] = jnp.broadcast_to((jnp.log2(total) + offset)[None], (copies, 1, 128))
    safe = jnp.logical_and(jnp.min(smallest) > SMALLEST, jnp.max(largest) < LARGEST)
    info_ref[:1, :] = jnp.broadcast_to(offset, (1, 128))
    info_ref[1:, :] = jnp.broadcast_to(jnp.where(safe, 1.0, 0.0), (1, 128))

    @pl.when(jnp.logical_not(safe))
    def _():
        def some_columns(c, _):
            own = pl.ds(pl.multiple_of(c * 128, 128), 128)
            ys = y_ref[own, :]

            def some_rows(r, state):
                top, total = state
                at = pl.ds(pl.multiple_of(r * 128, 128), 128)
                part = nt_dot(ys, x_ref[at, :]) * scale + rbias_ref[:, at]
                new = jnp.maximum(top, part)
                return new, total * jnp.exp2(top - new) + jnp.exp2(part - new)

            state = jnp.full((128, 128), -1e38, jnp.float32), jnp.zeros((128, 128), jnp.float32)
            top, total = lax.fori_loop(0, rows // 128, some_rows, state)
            best = jnp.max(top, axis=1, keepdims=True)
            total = jnp.sum(total * jnp.exp2(top - best), axis=1, keepdims=True)
            out_ref[:, :, own] = to_row(best + jnp.log2(total), copies)
            return 0

        lax.fori_loop(0, cols // 128, some_columns, 0)


def column_part(x, y, rbias, rsq, csq, scale, raised, copies=16):
    rows, depth = x.shape
    cols = y.shape[0]
    vmem = pl.BlockSpec(memory_space=pltpu.VMEM)
    return pl.pallas_call(
        functools.partial(column_kernel, scale, raised),
        in_specs=[vmem] * 5,
        out_specs=[vmem] * 4,
        out_shape=[
            jax.ShapeDtypeStruct((copies, 1, cols), jnp.float32),
            jax.ShapeDtypeStruct((rows // 2, cols), jnp.float32),
            jax.ShapeDtypeStruct((rows // 2, cols), jnp.float32),
            jax.ShapeDtypeStruct((2, 128), jnp.float32),
        ],
        scratch_shapes=[pltpu.VMEM((rows, 128), jnp.float32)] * 2,
        compiler_params=pltpu.CompilerParams(vmem_limit_bytes=8 * 2**20),
        cost_estimate=pl.CostEstimate(
            flops=2 * rows * cols * depth, bytes_accessed=2 * depth * (rows + cols), transcendentals=rows * cols
        ),
    )(x, y, rbias, rsq, csq)


def reward_kernel(
    scale, factor, n_cols, parts_ref, x_ref, y_ref, rbias_ref, rsq_ref, csq_ref, low_ref, high_ref, info_ref, out_ref, pot_ref, cbias_ref
):
    rows, cols = x_ref.shape[0], y_ref.shape[0]
    half = rows // 2
    best = functools.reduce(jnp.maximum, [parts_ref[i] for i in range(parts_ref.shape[0])])
    total = functools.reduce(jnp.add, [jnp.exp2(parts_ref[i] - best) for i in range(parts_ref.shape[0])])
    cbias_ref[...] = -(best + jnp.log2(total)) - math.log2(n_cols)
    potential = (cbias_ref[...] + scale * csq_ref[...]) * (EPS * LN2)
    size = cols // 16
    for b in range(16):
        place = (b % 4 * 4 + b // 4) * size
        pot_ref[:, place : place + size] = potential[:, b * size : (b + 1) * size]
    offset = jnp.max(info_ref[:1, :])
    far = jnp.min(cbias_ref[...]) + offset < HEADROOM_LIMIT
    usable = jnp.logical_and(jnp.min(info_ref[1:, :]) > 0.5, jnp.logical_not(far))

    @pl.when(usable)
    def _():
        gain = jnp.exp2(cbias_ref[...] + (offset + HEADROOM))
        for r in range(0, rows, 128):
            terms_ref, first, place = (low_ref, 0, r) if r < half else (high_ref, 8, r - half)
            total = jnp.zeros((128, 128), jnp.float32)
            for o in range(0, cols, 128):
                total = total + terms_ref[place : place + 128, o : o + 128] * gain[:, o : o + 128]
            value = to_row(jnp.sum(total, axis=1, keepdims=True), 8) * (factor * 2.0 ** (1.0 - HEADROOM) / scale)
            out_ref[first : first + 8, :, place : place + 128] = value

    @pl.when(jnp.logical_not(usable))
    def _():
        def some_rows(r, _):
            own = pl.ds(pl.multiple_of(r * 128, 128), 128)
            xs = x_ref[own, :]
            rbias = jnp.broadcast_to(rbias_ref[:, own], (128, 128)).T

            def some_columns(c, state):
                mass, moment = state
                at = pl.ds(pl.multiple_of(c * 128, 128), 128)
                part = nt_dot(xs, y_ref[at, :])
                plan = jnp.exp2((part * scale + cbias_ref[:, at]) + rbias)
                return mass + plan, moment + plan * (part - csq_ref[:, at])

            state = jnp.zeros((128, 128), jnp.float32), jnp.zeros((128, 128), jnp.float32)
            mass, moment = lax.fori_loop(0, cols // 128, some_columns, state)
            mass = to_row(jnp.sum(mass, axis=1, keepdims=True))
            moment = to_row(jnp.sum(moment, axis=1, keepdims=True))
            value = factor * (rsq_ref[:, own][None] * mass - 2.0 * moment)

            @pl.when(r < half // 128)
            def _():
                out_ref[:8, :, own] = jnp.broadcast_to(value, (8, 1, 128))

            @pl.when(r >= half // 128)
            def _():
                there = pl.ds(pl.multiple_of(r * 128 - half, 128), 128)
                out_ref[8:, :, there] = jnp.broadcast_to(value, (8, 1, 128))

            return 0

        lax.fori_loop(0, rows // 128, some_rows, 0)


def reward_part(parts, x, y, rbias, rsq, csq, low, high, info, scale, factor, n_cols):
    rows, cols = x.shape[0], y.shape[0]
    vmem = pl.BlockSpec(memory_space=pltpu.VMEM)
    return pl.pallas_call(
        functools.partial(reward_kernel, scale, factor, n_cols),
        in_specs=[vmem] * 9,
        out_specs=[vmem] * 2,
        out_shape=[
            jax.ShapeDtypeStruct((16, 1, rows // 2), jnp.float32),
            jax.ShapeDtypeStruct((1, cols), jnp.float32),
        ],
        scratch_shapes=[pltpu.VMEM((1, cols), jnp.float32)],
        compiler_params=pltpu.CompilerParams(vmem_limit_bytes=8 * 2**20),
        cost_estimate=pl.CostEstimate(flops=2 * rows * cols, bytes_accessed=4 * rows * cols, transcendentals=0),
    )(parts, x, y, rbias, rsq, csq, low, high, info)


def copy_kernel(in_ref, out_ref):
    out_ref[...] = jnp.broadcast_to(in_ref[...][None], out_ref.shape)


def copies(a, n):
    return pl.pallas_call(copy_kernel, out_shape=jax.ShapeDtypeStruct((n,) + a.shape, a.dtype))(a)


def swap(a, axis, bit, before):
    size = lax.axis_size(axis)
    other = lax.ppermute(a, axis, [(i, i ^ bit) for i in range(size)])
    low = (lax.axis_index(axis) & bit) == 0
    return jnp.stack([jnp.where(low, a, other), jnp.where(low, other, a)], axis=before)


def ring_gather(a, axes):
    n = math.prod(lax.axis_size(ax) for ax in axes)
    me = lax.axis_index(axes)
    zeros = (0,) * a.ndim

    def shift(v, by):
        return lax.ppermute(v, axes, [(i, (i + by) % n) for i in range(n)])

    def put(v, owner):
        return lax.dynamic_update_slice(out, v[None], (lax.rem(owner + n, n),) + zeros)

    out = jnp.zeros((n,) + a.shape, a.dtype)
    out = put(a, me)
    up = down = a
    for s in range(1, n // 2):
        up, down = shift(up, 1), shift(down, -1)
        out = put(up, me - s)
        out = put(down, me + s)
    return put(shift(up, 1), me - n // 2)


def merge(parts):
    parts = parts[:, 0]
    best = jnp.max(parts, axis=0)
    return best + jnp.log2(jnp.sum(jnp.exp2(parts - best), axis=0))


def body(logged, fresh, warm):
    depth = logged.shape[1]
    first = lax.axis_index("zh") == 0
    n_rows = logged.shape[0] * 256
    n_cols = fresh.shape[0] * 256

    many, logged, first = lax.optimization_barrier((copies(fresh, 16), logged, first))
    y = lax.all_to_all(many, COL_GROUP, 0, 0).reshape(-1, depth)
    x = swap(ring_gather(logged, ("zh", "zl")), "core", 1, 1).reshape(-1, depth)
    rows, cols = x.shape[0], y.shape[0]

    scale = 2.0 * LOG2E / (depth * EPS)
    xw = x.astype(jnp.float32)
    xsq = jnp.sum(xw * xw, axis=1)
    yw = y.astype(jnp.float32)
    ysq = jnp.sum(yw * yw, axis=1)
    warm = jnp.where(first, warm[:cols], warm[cols:]).reshape(4, 4, -1).transpose(1, 0, 2).reshape(-1)

    bias = warm * (LOG2E / EPS) - ysq * (0.5 * scale)
    part = lse(x, y, bias, scale, 1, 0.0)
    total = merge(lax.all_to_all(part, ROW_GROUP, 0, 0))
    rbias = -total - math.log2(n_rows)
    row_all = (rbias + xsq * (0.5 * scale)) * (EPS * LN2)

    part, low, high, info = column_part(x, y, rbias[None], xsq[None], (0.5 * ysq)[None], scale, 30.0)
    parts = lax.all_to_all(part, COL_GROUP, 0, 0)
    part, col_half = reward_part(
        parts, x, y, rbias[None], xsq[None], (0.5 * ysq)[None], low, high, info, scale, -n_rows / depth, n_cols
    )
    got = lax.all_to_all(part, ROW_GROUP, 0, 0)
    reward = jnp.sum(got[:, 0], axis=0)
    theirs = lax.ppermute(col_half, "zh", [(0, 1), (1, 0)])
    mine, theirs = col_half[0], theirs[0]
    col_potential = jnp.where(first, jnp.concatenate([mine, theirs]), jnp.concatenate([theirs, mine]))
    row_potential = jnp.where(first, row_all[: rows // 2], row_all[rows // 2 :])
    return row_potential, col_potential, reward


def solution(mesh):
    fine = Mesh(mesh.devices.reshape(2, 4, 4, 4, 2), AXES)
    return jax.shard_map(
        body,
        mesh=fine,
        in_specs=(P(AXES, None), P(("zl", "core", "zh", "y", "x"), None), P(("zl", "core"))),
        out_specs=(P(("zh", "y", "x")), P(("zl", "core")), P(("zh", "y", "x"))),
        check_vma=False,
    )
```

```python
import functools
import math

import jax
import jax.numpy as jnp
from jax import lax
from jax.experimental import pallas as pl
from jax.experimental.pallas import tpu as pltpu
from jax.sharding import Mesh
from jax.sharding import PartitionSpec as P

EPS = 0.01
AXES = ("zh", "y", "x", "zl", "core")
ROW_GROUP = ("zh", "core", "zl")
COL_GROUP = ("x", "y")
LN2 = math.log(2.0)
LOG2E = 1.0 / LN2


def nt_dot(a, b):
    return lax.dot_general(a, b, (((1,), (1,)), ((), ())), preferred_element_type=jnp.float32)


SAMPLE = 16
ROW_LARGEST, LARGEST, SMALLEST = 2.0**120, 2.0**112, 2.0**-100


def to_row(column, copies=1):
    row = jnp.broadcast_to(column, (column.shape[0], 128)).T[:1]
    return jnp.broadcast_to(row[None], (copies,) + row.shape)


def lse_kernel(scale, blocks, raised, x_ref, y_ref, bias_ref, few_ref, out_ref, moved_ref):
    rows, cols = x_ref.shape[0], y_ref.shape[0]
    copies = out_ref.shape[0]
    step = rows // 16
    some = jnp.concatenate([x_ref[s : s + 2 * SAMPLE, :] for s in range(0, rows, step)], axis=0)
    step = cols // 16
    few = jnp.concatenate([y_ref[s : s + SAMPLE, :] for s in range(0, cols, step)], axis=0)
    seen = nt_dot(some, few) * scale + few_ref[...]
    seen = jnp.maximum(seen[:, :128], seen[:, 128:]).reshape(blocks, -1, 128)
    offset = jnp.max(jnp.max(seen, axis=1), axis=1, keepdims=True) - raised
    moved_ref[...] = bias_ref[...] - offset

    size = rows // blocks
    totals = [jnp.zeros((size, 128), jnp.float32)] * blocks
    for start in range(0, cols, 256):
        prod = nt_dot(x_ref[...], y_ref[start : start + 256, :])
        for b in range(blocks):
            for o in (0, 128):
                part = prod[b * size : (b + 1) * size, o : o + 128]
                at = slice(start + o, start + o + 128)
                totals[b] = totals[b] + jnp.exp2(part * scale + moved_ref[b : b + 1, at])
    safe = None
    for b in range(blocks):
        total = jnp.sum(totals[b], axis=1, keepdims=True)
        value = jnp.log2(total) + offset[b : b + 1, :]
        out_ref[:, :, b * size : (b + 1) * size] = to_row(value, copies)
        good = jnp.logical_and(jnp.min(total) > SMALLEST, jnp.max(total) < ROW_LARGEST)
        safe = good if safe is None else jnp.logical_and(safe, good)

    @pl.when(jnp.logical_not(safe))
    def _():
        def some_rows(r, _):
            own = pl.ds(pl.multiple_of(r * 128, 128), 128)
            xs = x_ref[own, :]

            def some_columns(c, state):
                top, total = state
                at = pl.ds(pl.multiple_of(c * 128, 128), 128)
                part = nt_dot(xs, y_ref[at, :]) * scale + bias_ref[:, at]
                new = jnp.maximum(top, part)
                return new, total * jnp.exp2(top - new) + jnp.exp2(part - new)

            state = jnp.full((128, 128), -1e38, jnp.float32), jnp.zeros((128, 128), jnp.float32)
            top, total = lax.fori_loop(0, cols // 128, some_columns, state)
            best = jnp.max(top, axis=1, keepdims=True)
            total = jnp.sum(total * jnp.exp2(top - best), axis=1, keepdims=True)
            out_ref[:, :, own] = to_row(best + jnp.log2(total), copies)
            return 0

        lax.fori_loop(0, rows // 128, some_rows, 0)


def lse(x, y, bias, scale, blocks, raised, copies=16):
    rows, depth = x.shape
    cols = y.shape[0]
    few = bias.reshape(16, cols // 16)[:, :SAMPLE].reshape(1, 16 * SAMPLE)
    return pl.pallas_call(
        functools.partial(lse_kernel, scale, blocks, raised),
        out_shape=jax.ShapeDtypeStruct((copies, 1, rows), jnp.float32),
        scratch_shapes=[pltpu.VMEM((blocks, cols), jnp.float32)],
        compiler_params=pltpu.CompilerParams(vmem_limit_bytes=40 * 2**20),
        cost_estimate=pl.CostEstimate(
            flops=2 * rows * cols * depth, bytes_accessed=2 * depth * (rows + cols), transcendentals=rows * cols
        ),
    )(x, y, bias.reshape(1, cols), few)


def over_lanes(row):
    high = row.astype(jnp.bfloat16)
    rest = row - high.astype(jnp.float32)
    mid = rest.astype(jnp.bfloat16)
    low = (rest - mid.astype(jnp.float32)).astype(jnp.bfloat16)
    parts = jnp.concatenate([high, mid, low, jnp.zeros((13, row.shape[1]), jnp.bfloat16)], axis=0)
    ones = jnp.ones((16, 128), jnp.bfloat16)
    return lax.dot_general(parts, ones, (((0,), (0,)), ((), ())), preferred_element_type=jnp.float32)


def fold(a, height):
    return jnp.sum(a.reshape(a.shape[0] // height, height, a.shape[1]), axis=0)


MB = 512
HEADROOM = 40.0
HEADROOM_LIMIT = -160.0


def column_kernel(scale, raised, x_ref, y_ref, rbias_ref, rsq_ref, csq_ref, out_ref, low_ref, high_ref, info_ref, wide_ref, pot_ref):
    rows, cols = x_ref.shape[0], y_ref.shape[0]
    copies = out_ref.shape[0]
    wide_ref[...] = over_lanes(rbias_ref[...])
    step = cols // 16
    some = jnp.concatenate([y_ref[s : s + 2 * SAMPLE, :] for s in range(0, cols, step)], axis=0)
    step = rows // 16
    few = jnp.concatenate([x_ref[s : s + SAMPLE, :] for s in range(0, rows, step)], axis=0)
    few_bias = jnp.concatenate([wide_ref[s : s + SAMPLE, :] for s in range(0, rows, step)], axis=0)
    seen = nt_dot(few, some)
    seen = functools.reduce(jnp.maximum, [seen[:, o : o + 128] * scale + few_bias for o in range(0, 512, 128)])
    offset = jnp.max(jnp.max(seen, axis=0, keepdims=True), axis=1, keepdims=True) - raised
    wide_ref[...] = wide_ref[...] - offset
    pot_ref[...] = over_lanes(rbias_ref[...] + (0.5 * scale) * rsq_ref[...] - offset)

    smallest = largest = None
    for t in range(0, cols, 256):
        totals = [jnp.zeros((32, 128), jnp.float32)] * 2
        for start in range(0, rows, MB):
            prod = nt_dot(x_ref[start : start + MB, :], y_ref[t : t + 256, :])
            wide = wide_ref[start : start + MB, :]
            pot = pot_ref[start : start + MB, :]
            for b in (0, 1):
                at = slice(t + b * 128, t + b * 128 + 128)
                power = prod[:, b * 128 : b * 128 + 128] * scale + wide
                term = jnp.exp2(power)
                totals[b] = totals[b] + fold(term, 32)
                terms_ref = low_ref if start < rows // 2 else high_ref
                place = start % (rows // 2)
                terms_ref[place : place + MB, at] = term * ((scale * csq_ref[:, at] - power) + pot)
        for b in (0, 1):
            total = jnp.sum(totals[b], axis=0, keepdims=True)
            smallest = total if smallest is None else jnp.minimum(smallest, total)
            largest = total if largest is None else jnp.maximum(largest, total)
            at = slice(t + b * 128, t + b * 128 + 128)
            out_ref[:, :, at] = jnp.broadcast_to((jnp.log2(total) + offset)[None], (copies, 1, 128))
    safe = jnp.logical_and(jnp.min(smallest) > SMALLEST, jnp.max(largest) < LARGEST)
    info_ref[:1, :] = jnp.broadcast_to(offset, (1, 128))
    info_ref[1:, :] = jnp.broadcast_to(jnp.where(safe, 1.0, 0.0), (1, 128))

    @pl.when(jnp.logical_not(safe))
    def _():
        def some_columns(c, _):
            own = pl.ds(pl.multiple_of(c * 128, 128), 128)
            ys = y_ref[own, :]

            def some_rows(r, state):
                top, total = state
                at = pl.ds(pl.multiple_of(r * 128, 128), 128)
                part = nt_dot(ys, x_ref[at, :]) * scale + rbias_ref[:, at]
                new = jnp.maximum(top, part)
                return new, total * jnp.exp2(top - new) + jnp.exp2(part - new)

            state = jnp.full((128, 128), -1e38, jnp.float32), jnp.zeros((128, 128), jnp.float32)
            top, total = lax.fori_loop(0, rows // 128, some_rows, state)
            best = jnp.max(top, axis=1, keepdims=True)
            total = jnp.sum(total * jnp.exp2(top - best), axis=1, keepdims=True)
            out_ref[:, :, own] = to_row(best + jnp.log2(total), copies)
            return 0

        lax.fori_loop(0, cols // 128, some_columns, 0)


def column_part(x, y, rbias, rsq, csq, scale, raised, copies=16):
    rows, depth = x.shape
    cols = y.shape[0]
    vmem = pl.BlockSpec(memory_space=pltpu.VMEM)
    return pl.pallas_call(
        functools.partial(column_kernel, scale, raised),
        in_specs=[vmem] * 5,
        out_specs=[vmem] * 4,
        out_shape=[
            jax.ShapeDtypeStruct((copies, 1, cols), jnp.float32),
            jax.ShapeDtypeStruct((rows // 2, cols), jnp.float32),
            jax.ShapeDtypeStruct((rows // 2, cols), jnp.float32),
            jax.ShapeDtypeStruct((2, 128), jnp.float32),
        ],
        scratch_shapes=[pltpu.VMEM((rows, 128), jnp.float32)] * 2,
        compiler_params=pltpu.CompilerParams(vmem_limit_bytes=8 * 2**20),
        cost_estimate=pl.CostEstimate(
            flops=2 * rows * cols * depth, bytes_accessed=2 * depth * (rows + cols), transcendentals=rows * cols
        ),
    )(x, y, rbias, rsq, csq)


def reward_kernel(
    scale, factor, n_cols, parts_ref, x_ref, y_ref, rbias_ref, rsq_ref, csq_ref, low_ref, high_ref, info_ref, out_ref, pot_ref, cbias_ref
):
    rows, cols = x_ref.shape[0], y_ref.shape[0]
    half = rows // 2
    best = functools.reduce(jnp.maximum, [parts_ref[i] for i in range(parts_ref.shape[0])])
    total = functools.reduce(jnp.add, [jnp.exp2(parts_ref[i] - best) for i in range(parts_ref.shape[0])])
    cbias_ref[...] = -(best + jnp.log2(total)) - math.log2(n_cols)
    potential = (cbias_ref[...] + scale * csq_ref[...]) * (EPS * LN2)
    size = cols // 16
    for b in range(16):
        place = (b % 4 * 4 + b // 4) * size
        pot_ref[:, place : place + size] = potential[:, b * size : (b + 1) * size]
    offset = jnp.max(info_ref[:1, :])
    far = jnp.min(cbias_ref[...]) + offset < HEADROOM_LIMIT
    usable = jnp.logical_and(jnp.min(info_ref[1:, :]) > 0.5, jnp.logical_not(far))

    @pl.when(usable)
    def _():
        gain = jnp.exp2(cbias_ref[...] + (offset + HEADROOM))
        for r in range(0, rows, 128):
            terms_ref, first, place = (low_ref, 0, r) if r < half else (high_ref, 8, r - half)
            total = jnp.zeros((128, 128), jnp.float32)
            for o in range(0, cols, 128):
                total = total + terms_ref[place : place + 128, o : o + 128] * gain[:, o : o + 128]
            value = to_row(jnp.sum(total, axis=1, keepdims=True), 8) * (factor * 2.0 ** (1.0 - HEADROOM) / scale)
            out_ref[first : first + 8, :, place : place + 128] = value

    @pl.when(jnp.logical_not(usable))
    def _():
        def some_rows(r, _):
            own = pl.ds(pl.multiple_of(r * 128, 128), 128)
            xs = x_ref[own, :]
            rbias = jnp.broadcast_to(rbias_ref[:, own], (128, 128)).T

            def some_columns(c, state):
                mass, moment = state
                at = pl.ds(pl.multiple_of(c * 128, 128), 128)
                part = nt_dot(xs, y_ref[at, :])
                plan = jnp.exp2((part * scale + cbias_ref[:, at]) + rbias)
                return mass + plan, moment + plan * (part - csq_ref[:, at])

            state = jnp.zeros((128, 128), jnp.float32), jnp.zeros((128, 128), jnp.float32)
            mass, moment = lax.fori_loop(0, cols // 128, some_columns, state)
            mass = to_row(jnp.sum(mass, axis=1, keepdims=True))
            moment = to_row(jnp.sum(moment, axis=1, keepdims=True))
            value = factor * (rsq_ref[:, own][None] * mass - 2.0 * moment)

            @pl.when(r < half // 128)
            def _():
                out_ref[:8, :, own] = jnp.broadcast_to(value, (8, 1, 128))

            @pl.when(r >= half // 128)
            def _():
                there = pl.ds(pl.multiple_of(r * 128 - half, 128), 128)
                out_ref[8:, :, there] = jnp.broadcast_to(value, (8, 1, 128))

            return 0

        lax.fori_loop(0, rows // 128, some_rows, 0)


def reward_part(parts, x, y, rbias, rsq, csq, low, high, info, scale, factor, n_cols):
    rows, cols = x.shape[0], y.shape[0]
    vmem = pl.BlockSpec(memory_space=pltpu.VMEM)
    return pl.pallas_call(
        functools.partial(reward_kernel, scale, factor, n_cols),
        in_specs=[vmem] * 9,
        out_specs=[vmem] * 2,
        out_shape=[
            jax.ShapeDtypeStruct((16, 1, rows // 2), jnp.float32),
            jax.ShapeDtypeStruct((1, cols), jnp.float32),
        ],
        scratch_shapes=[pltpu.VMEM((1, cols), jnp.float32)],
        compiler_params=pltpu.CompilerParams(vmem_limit_bytes=8 * 2**20),
        cost_estimate=pl.CostEstimate(flops=2 * rows * cols, bytes_accessed=4 * rows * cols, transcendentals=0),
    )(parts, x, y, rbias, rsq, csq, low, high, info)


def copy_kernel(in_ref, out_ref):
    out_ref[...] = jnp.broadcast_to(in_ref[...][None], out_ref.shape)


def copies(a, n):
    return pl.pallas_call(copy_kernel, out_shape=jax.ShapeDtypeStruct((n,) + a.shape, a.dtype))(a)


def swap(a, axis, bit, before):
    size = lax.axis_size(axis)
    other = lax.ppermute(a, axis, [(i, i ^ bit) for i in range(size)])
    low = (lax.axis_index(axis) & bit) == 0
    return jnp.stack([jnp.where(low, a, other), jnp.where(low, other, a)], axis=before)


def ring_gather(a, axes):
    n = math.prod(lax.axis_size(ax) for ax in axes)
    me = lax.axis_index(axes)
    zeros = (0,) * a.ndim

    def shift(v, by):
        return lax.ppermute(v, axes, [(i, (i + by) % n) for i in range(n)])

    def put(v, owner):
        return lax.dynamic_update_slice(out, v[None], (lax.rem(owner + n, n),) + zeros)

    out = jnp.zeros((n,) + a.shape, a.dtype)
    out = put(a, me)
    up = down = a
    for s in range(1, n // 2):
        up, down = shift(up, 1), shift(down, -1)
        out = put(up, me - s)
        out = put(down, me + s)
    return put(shift(up, 1), me - n // 2)


def merge(parts):
    parts = parts[:, 0]
    best = jnp.max(parts, axis=0)
    return best + jnp.log2(jnp.sum(jnp.exp2(parts - best), axis=0))


def body(logged, fresh, warm):
    depth = logged.shape[1]
    first = lax.axis_index("zh") == 0
    n_rows = logged.shape[0] * 256
    n_cols = fresh.shape[0] * 256

    many, logged, first = lax.optimization_barrier((copies(fresh, 16), logged, first))
    y = lax.all_to_all(many, COL_GROUP, 0, 0).reshape(-1, depth)
    x = swap(ring_gather(logged, ("zh", "zl")), "core", 1, 1).reshape(-1, depth)
    rows, cols = x.shape[0], y.shape[0]

    scale = 2.0 * LOG2E / (depth * EPS)
    xw = x.astype(jnp.float32)
    xsq = jnp.sum(xw * xw, axis=1)
    yw = y.astype(jnp.float32)
    ysq = jnp.sum(yw * yw, axis=1)
    warm = jnp.where(first, warm[:cols], warm[cols:]).reshape(4, 4, -1).transpose(1, 0, 2).reshape(-1)

    bias = warm * (LOG2E / EPS) - ysq * (0.5 * scale)
    part = lse(x, y, bias, scale, 1, -14.0)
    total = merge(lax.all_to_all(part, ROW_GROUP, 0, 0))
    rbias = -total - math.log2(n_rows)
    row_all = (rbias + xsq * (0.5 * scale)) * (EPS * LN2)

    part, low, high, info = column_part(x, y, rbias[None], xsq[None], (0.5 * ysq)[None], scale, 25.0)
    parts = lax.all_to_all(part, COL_GROUP, 0, 0)
    part, col_half = reward_part(
        parts, x, y, rbias[None], xsq[None], (0.5 * ysq)[None], low, high, info, scale, -n_rows / depth, n_cols
    )
    got = lax.all_to_all(part, ROW_GROUP, 0, 0)
    reward = jnp.sum(got[:, 0], axis=0)
    theirs = lax.ppermute(col_half, "zh", [(0, 1), (1, 0)])
    reward, theirs = lax.optimization_barrier((reward, theirs))
    mine, theirs = col_half[0], theirs[0]
    col_potential = jnp.where(first, jnp.concatenate([mine, theirs]), jnp.concatenate([theirs, mine]))
    row_potential = jnp.where(first, row_all[: rows // 2], row_all[rows // 2 :])
    return row_potential, col_potential, reward


def solution(mesh):
    fine = Mesh(mesh.devices.reshape(2, 4, 4, 4, 2), AXES)
    return jax.shard_map(
        body,
        mesh=fine,
        in_specs=(P(AXES, None), P(("zl", "core", "zh", "y", "x"), None), P(("zl", "core"))),
        out_specs=(P(("zh", "y", "x")), P(("zl", "core")), P(("zh", "y", "x"))),
        check_vma=False,
    )
```

```python
import functools
import math

import jax
import jax.numpy as jnp
from jax import lax
from jax.experimental import pallas as pl
from jax.experimental.pallas import tpu as pltpu
from jax.sharding import Mesh
from jax.sharding import PartitionSpec as P

EPS = 0.01
AXES = ("zh", "y", "x", "zl", "core")
ROW_GROUP = ("zh", "core", "zl")
COL_GROUP = ("x", "y")
LN2 = math.log(2.0)
LOG2E = 1.0 / LN2


def nt_dot(a, b):
    return lax.dot_general(a, b, (((1,), (1,)), ((), ())), preferred_element_type=jnp.float32)


SAMPLE = 16
ROW_LARGEST, LARGEST, SMALLEST = 2.0**120, 2.0**112, 2.0**-100


def to_row(column, copies=1):
    row = jnp.broadcast_to(column, (column.shape[0], 128)).T[:1]
    return jnp.broadcast_to(row[None], (copies,) + row.shape)


def lse_kernel(scale, blocks, raised, x_ref, y_ref, bias_ref, few_ref, out_ref, moved_ref):
    rows, cols = x_ref.shape[0], y_ref.shape[0]
    copies = out_ref.shape[0]
    step = rows // 16
    some = jnp.concatenate([x_ref[s : s + 2 * SAMPLE, :] for s in range(0, rows, step)], axis=0)
    step = cols // 16
    few = jnp.concatenate([y_ref[s : s + SAMPLE, :] for s in range(0, cols, step)], axis=0)
    seen = nt_dot(some, few) * scale + few_ref[...]
    seen = jnp.maximum(seen[:, :128], seen[:, 128:]).reshape(blocks, -1, 128)
    offset = jnp.max(jnp.max(seen, axis=1), axis=1, keepdims=True) - raised
    moved_ref[...] = bias_ref[...] - offset

    size = rows // blocks
    totals = [jnp.zeros((size, 128), jnp.float32)] * blocks
    for start in range(0, cols, 256):
        prod = nt_dot(x_ref[...], y_ref[start : start + 256, :])
        for b in range(blocks):
            for o in (0, 128):
                part = prod[b * size : (b + 1) * size, o : o + 128]
                at = slice(start + o, start + o + 128)
                totals[b] = totals[b] + jnp.exp2(part * scale + moved_ref[b : b + 1, at])
    safe = None
    for b in range(blocks):
        total = jnp.sum(totals[b], axis=1, keepdims=True)
        value = jnp.log2(total) + offset[b : b + 1, :]
        out_ref[:, :, b * size : (b + 1) * size] = to_row(value, copies)
        good = jnp.logical_and(jnp.min(total) > SMALLEST, jnp.max(total) < ROW_LARGEST)
        safe = good if safe is None else jnp.logical_and(safe, good)

    @pl.when(jnp.logical_not(safe))
    def _():
        def some_rows(r, _):
            own = pl.ds(pl.multiple_of(r * 128, 128), 128)
            xs = x_ref[own, :]

            def some_columns(c, state):
                top, total = state
                at = pl.ds(pl.multiple_of(c * 128, 128), 128)
                part = nt_dot(xs, y_ref[at, :]) * scale + bias_ref[:, at]
                new = jnp.maximum(top, part)
                return new, total * jnp.exp2(top - new) + jnp.exp2(part - new)

            state = jnp.full((128, 128), -1e38, jnp.float32), jnp.zeros((128, 128), jnp.float32)
            top, total = lax.fori_loop(0, cols // 128, some_columns, state)
            best = jnp.max(top, axis=1, keepdims=True)
            total = jnp.sum(total * jnp.exp2(top - best), axis=1, keepdims=True)
            out_ref[:, :, own] = to_row(best + jnp.log2(total), copies)
            return 0

        lax.fori_loop(0, rows // 128, some_rows, 0)


def lse(x, y, bias, scale, blocks, raised, copies=16):
    rows, depth = x.shape
    cols = y.shape[0]
    few = bias.reshape(16, cols // 16)[:, :SAMPLE].reshape(1, 16 * SAMPLE)
    return pl.pallas_call(
        functools.partial(lse_kernel, scale, blocks, raised),
        out_shape=jax.ShapeDtypeStruct((copies, 1, rows), jnp.float32),
        scratch_shapes=[pltpu.VMEM((blocks, cols), jnp.float32)],
        compiler_params=pltpu.CompilerParams(vmem_limit_bytes=40 * 2**20),
        cost_estimate=pl.CostEstimate(
            flops=2 * rows * cols * depth, bytes_accessed=2 * depth * (rows + cols), transcendentals=rows * cols
        ),
    )(x, y, bias.reshape(1, cols), few)


def over_lanes(row):
    high = row.astype(jnp.bfloat16)
    rest = row - high.astype(jnp.float32)
    mid = rest.astype(jnp.bfloat16)
    low = (rest - mid.astype(jnp.float32)).astype(jnp.bfloat16)
    parts = jnp.concatenate([high, mid, low, jnp.zeros((13, row.shape[1]), jnp.bfloat16)], axis=0)
    ones = jnp.ones((16, 128), jnp.bfloat16)
    return lax.dot_general(parts, ones, (((0,), (0,)), ((), ())), preferred_element_type=jnp.float32)


def fold(a, height):
    return jnp.sum(a.reshape(a.shape[0] // height, height, a.shape[1]), axis=0)


MB = 512
HEADROOM = 40.0
HEADROOM_LIMIT = -160.0


def column_kernel(scale, raised, x_ref, y_ref, rbias_ref, rsq_ref, csq_ref, out_ref, low_ref, high_ref, info_ref, wide_ref, pot_ref, row_ref):
    rows, cols = x_ref.shape[0], y_ref.shape[0]
    copies = out_ref.shape[0]
    wide_ref[...] = over_lanes(rbias_ref[...])
    pot_ref[...] = over_lanes(rbias_ref[...] + (0.5 * scale) * rsq_ref[...])
    step = cols // 16
    some = jnp.concatenate([y_ref[s : s + 2 * SAMPLE, :] for s in range(0, cols, step)], axis=0)
    step = rows // 16
    few = jnp.concatenate([x_ref[s : s + SAMPLE, :] for s in range(0, rows, step)], axis=0)
    few_bias = jnp.concatenate([wide_ref[s : s + SAMPLE, :] for s in range(0, rows, step)], axis=0)
    seen = nt_dot(few, some)
    seen = functools.reduce(jnp.maximum, [seen[:, o : o + 128] * scale + few_bias for o in range(0, 512, 128)])
    offset = jnp.max(jnp.max(seen, axis=0, keepdims=True), axis=1, keepdims=True) - raised
    wide_ref[...] = wide_ref[...] - offset
    row_ref[...] = scale * csq_ref[...] - offset

    smallest = largest = None
    for t in range(0, cols, 256):
        totals = [jnp.zeros((32, 128), jnp.float32)] * 2
        for start in range(0, rows, MB):
            prod = nt_dot(x_ref[start : start + MB, :], y_ref[t : t + 256, :])
            wide = wide_ref[start : start + MB, :]
            pot = pot_ref[start : start + MB, :]
            for b in (0, 1):
                at = slice(t + b * 128, t + b * 128 + 128)
                power = prod[:, b * 128 : b * 128 + 128] * scale + wide
                term = jnp.exp2(power)
                totals[b] = totals[b] + fold(term, 32)
                terms_ref = low_ref if start < rows // 2 else high_ref
                place = start % (rows // 2)
                terms_ref[place : place + MB, at] = term * ((row_ref[:, at] - power) + pot)
        for b in (0, 1):
            total = jnp.sum(totals[b], axis=0, keepdims=True)
            smallest = total if smallest is None else jnp.minimum(smallest, total)
            largest = total if largest is None else jnp.maximum(largest, total)
            at = slice(t + b * 128, t + b * 128 + 128)
            out_ref[:, :, at] = jnp.broadcast_to((jnp.log2(total) + offset)[None], (copies, 1, 128))
    safe = jnp.logical_and(jnp.min(smallest) > SMALLEST, jnp.max(largest) < LARGEST)
    info_ref[:1, :] = jnp.broadcast_to(offset, (1, 128))
    info_ref[1:, :] = jnp.broadcast_to(jnp.where(safe, 1.0, 0.0), (1, 128))

    @pl.when(jnp.logical_not(safe))
    def _():
        def some_columns(c, _):
            own = pl.ds(pl.multiple_of(c * 128, 128), 128)
            ys = y_ref[own, :]

            def some_rows(r, state):
                top, total = state
                at = pl.ds(pl.multiple_of(r * 128, 128), 128)
                part = nt_dot(ys, x_ref[at, :]) * scale + rbias_ref[:, at]
                new = jnp.maximum(top, part)
                return new, total * jnp.exp2(top - new) + jnp.exp2(part - new)

            state = jnp.full((128, 128), -1e38, jnp.float32), jnp.zeros((128, 128), jnp.float32)
            top, total = lax.fori_loop(0, rows // 128, some_rows, state)
            best = jnp.max(top, axis=1, keepdims=True)
            total = jnp.sum(total * jnp.exp2(top - best), axis=1, keepdims=True)
            out_ref[:, :, own] = to_row(best + jnp.log2(total), copies)
            return 0

        lax.fori_loop(0, cols // 128, some_columns, 0)


def column_part(x, y, rbias, rsq, csq, scale, raised, copies=16):
    rows, depth = x.shape
    cols = y.shape[0]
    vmem = pl.BlockSpec(memory_space=pltpu.VMEM)
    return pl.pallas_call(
        functools.partial(column_kernel, scale, raised),
        in_specs=[vmem] * 5,
        out_specs=[vmem] * 4,
        out_shape=[
            jax.ShapeDtypeStruct((copies, 1, cols), jnp.float32),
            jax.ShapeDtypeStruct((rows // 2, cols), jnp.float32),
            jax.ShapeDtypeStruct((rows // 2, cols), jnp.float32),
            jax.ShapeDtypeStruct((2, 128), jnp.float32),
        ],
        scratch_shapes=[pltpu.VMEM((rows, 128), jnp.float32)] * 2 + [pltpu.VMEM((1, cols), jnp.float32)],
        compiler_params=pltpu.CompilerParams(vmem_limit_bytes=8 * 2**20),
        cost_estimate=pl.CostEstimate(
            flops=2 * rows * cols * depth, bytes_accessed=2 * depth * (rows + cols), transcendentals=rows * cols
        ),
    )(x, y, rbias, rsq, csq)


def reward_kernel(
    scale, factor, n_cols, parts_ref, x_ref, y_ref, rbias_ref, rsq_ref, csq_ref, low_ref, high_ref, info_ref, out_ref, pot_ref, cbias_ref
):
    rows, cols = x_ref.shape[0], y_ref.shape[0]
    half = rows // 2
    best = functools.reduce(jnp.maximum, [parts_ref[i] for i in range(parts_ref.shape[0])])
    total = functools.reduce(jnp.add, [jnp.exp2(parts_ref[i] - best) for i in range(parts_ref.shape[0])])
    cbias_ref[...] = -(best + jnp.log2(total)) - math.log2(n_cols)
    potential = (cbias_ref[...] + scale * csq_ref[...]) * (EPS * LN2)
    size = cols // 16
    for b in range(16):
        place = (b % 4 * 4 + b // 4) * size
        pot_ref[:, place : place + size] = potential[:, b * size : (b + 1) * size]
    offset = jnp.max(info_ref[:1, :])
    far = jnp.min(cbias_ref[...]) + offset < HEADROOM_LIMIT
    usable = jnp.logical_and(jnp.min(info_ref[1:, :]) > 0.5, jnp.logical_not(far))

    @pl.when(usable)
    def _():
        gain = jnp.exp2(cbias_ref[...] + (offset + HEADROOM))
        for r in range(0, rows, 128):
            terms_ref, first, place = (low_ref, 0, r) if r < half else (high_ref, 8, r - half)
            total = jnp.zeros((128, 128), jnp.float32)
            for o in range(0, cols, 128):
                total = total + terms_ref[place : place + 128, o : o + 128] * gain[:, o : o + 128]
            value = to_row(jnp.sum(total, axis=1, keepdims=True), 8) * (factor * 2.0 ** (1.0 - HEADROOM) / scale)
            out_ref[first : first + 8, :, place : place + 128] = value

    @pl.when(jnp.logical_not(usable))
    def _():
        def some_rows(r, _):
            own = pl.ds(pl.multiple_of(r * 128, 128), 128)
            xs = x_ref[own, :]
            rbias = jnp.broadcast_to(rbias_ref[:, own], (128, 128)).T

            def some_columns(c, state):
                mass, moment = state
                at = pl.ds(pl.multiple_of(c * 128, 128), 128)
                part = nt_dot(xs, y_ref[at, :])
                plan = jnp.exp2((part * scale + cbias_ref[:, at]) + rbias)
                return mass + plan, moment + plan * (part - csq_ref[:, at])

            state = jnp.zeros((128, 128), jnp.float32), jnp.zeros((128, 128), jnp.float32)
            mass, moment = lax.fori_loop(0, cols // 128, some_columns, state)
            mass = to_row(jnp.sum(mass, axis=1, keepdims=True))
            moment = to_row(jnp.sum(moment, axis=1, keepdims=True))
            value = factor * (rsq_ref[:, own][None] * mass - 2.0 * moment)

            @pl.when(r < half // 128)
            def _():
                out_ref[:8, :, own] = jnp.broadcast_to(value, (8, 1, 128))

            @pl.when(r >= half // 128)
            def _():
                there = pl.ds(pl.multiple_of(r * 128 - half, 128), 128)
                out_ref[8:, :, there] = jnp.broadcast_to(value, (8, 1, 128))

            return 0

        lax.fori_loop(0, rows // 128, some_rows, 0)


def reward_part(parts, x, y, rbias, rsq, csq, low, high, info, scale, factor, n_cols):
    rows, cols = x.shape[0], y.shape[0]
    vmem = pl.BlockSpec(memory_space=pltpu.VMEM)
    return pl.pallas_call(
        functools.partial(reward_kernel, scale, factor, n_cols),
        in_specs=[vmem] * 9,
        out_specs=[vmem] * 2,
        out_shape=[
            jax.ShapeDtypeStruct((16, 1, rows // 2), jnp.float32),
            jax.ShapeDtypeStruct((1, cols), jnp.float32),
        ],
        scratch_shapes=[pltpu.VMEM((1, cols), jnp.float32)],
        compiler_params=pltpu.CompilerParams(vmem_limit_bytes=8 * 2**20),
        cost_estimate=pl.CostEstimate(flops=2 * rows * cols, bytes_accessed=4 * rows * cols, transcendentals=0),
    )(parts, x, y, rbias, rsq, csq, low, high, info)


def copy_kernel(in_ref, out_ref):
    out_ref[...] = jnp.broadcast_to(in_ref[...][None], out_ref.shape)


def copies(a, n):
    return pl.pallas_call(copy_kernel, out_shape=jax.ShapeDtypeStruct((n,) + a.shape, a.dtype))(a)


def swap(a, axis, bit, before):
    size = lax.axis_size(axis)
    other = lax.ppermute(a, axis, [(i, i ^ bit) for i in range(size)])
    low = (lax.axis_index(axis) & bit) == 0
    return jnp.stack([jnp.where(low, a, other), jnp.where(low, other, a)], axis=before)


def ring_gather(a, axes):
    n = math.prod(lax.axis_size(ax) for ax in axes)
    me = lax.axis_index(axes)
    zeros = (0,) * a.ndim

    def shift(v, by):
        return lax.ppermute(v, axes, [(i, (i + by) % n) for i in range(n)])

    def put(v, owner):
        return lax.dynamic_update_slice(out, v[None], (lax.rem(owner + n, n),) + zeros)

    out = jnp.zeros((n,) + a.shape, a.dtype)
    out = put(a, me)
    up = down = a
    for s in range(1, n // 2):
        up, down = shift(up, 1), shift(down, -1)
        out = put(up, me - s)
        out = put(down, me + s)
    return put(shift(up, 1), me - n // 2)


def merge(parts):
    parts = parts[:, 0]
    best = jnp.max(parts, axis=0)
    return best + jnp.log2(jnp.sum(jnp.exp2(parts - best), axis=0))


def body(logged, fresh, warm):
    depth = logged.shape[1]
    first = lax.axis_index("zh") == 0
    n_rows = logged.shape[0] * 256
    n_cols = fresh.shape[0] * 256

    many, logged, first = lax.optimization_barrier((copies(fresh, 16), logged, first))
    y = lax.all_to_all(many, COL_GROUP, 0, 0).reshape(-1, depth)
    x = swap(ring_gather(logged, ("zh", "zl")), "core", 1, 1).reshape(-1, depth)
    rows, cols = x.shape[0], y.shape[0]

    scale = 2.0 * LOG2E / (depth * EPS)
    xw = x.astype(jnp.float32)
    xsq = jnp.sum(xw * xw, axis=1)
    yw = y.astype(jnp.float32)
    ysq = jnp.sum(yw * yw, axis=1)
    warm = jnp.where(first, warm[:cols], warm[cols:]).reshape(4, 4, -1).transpose(1, 0, 2).reshape(-1)

    bias = warm * (LOG2E / EPS) - ysq * (0.5 * scale)
    part = lse(x, y, bias, scale, 1, -14.0)
    total = merge(lax.all_to_all(part, ROW_GROUP, 0, 0))
    rbias = -total - math.log2(n_rows)
    row_all = (rbias + xsq * (0.5 * scale)) * (EPS * LN2)

    part, low, high, info = column_part(x, y, rbias[None], xsq[None], (0.5 * ysq)[None], scale, 25.0)
    parts = lax.all_to_all(part, COL_GROUP, 0, 0)
    part, col_half = reward_part(
        parts, x, y, rbias[None], xsq[None], (0.5 * ysq)[None], low, high, info, scale, -n_rows / depth, n_cols
    )
    got = lax.all_to_all(part, ROW_GROUP, 0, 0)
    reward = jnp.sum(got[:, 0], axis=0)
    theirs = lax.ppermute(col_half, "zh", [(0, 1), (1, 0)])
    reward, theirs = lax.optimization_barrier((reward, theirs))
    mine, theirs = col_half[0], theirs[0]
    col_potential = jnp.where(first, jnp.concatenate([mine, theirs]), jnp.concatenate([theirs, mine]))
    row_potential = jnp.where(first, row_all[: rows // 2], row_all[rows // 2 :])
    return row_potential, col_potential, reward


def solution(mesh):
    fine = Mesh(mesh.devices.reshape(2, 4, 4, 4, 2), AXES)
    return jax.shard_map(
        body,
        mesh=fine,
        in_specs=(P(AXES, None), P(("zl", "core", "zh", "y", "x"), None), P(("zl", "core"))),
        out_specs=(P(("zh", "y", "x")), P(("zl", "core")), P(("zh", "y", "x"))),
        check_vma=False,
    )
```
